256 devices in a mesh: tm: 8 (over x, core), space: 32 (over y, z).
Axes of the slice: x: 4, y: 4, z: 8, core: 2. Of those that a mesh axis runs over, the one named last changes fastest.
Arguments:
- guess: float32 [8, 16, 2048, 128], P('tm', None, 'space'), may hold values from -6 to 6
- coeffs: bfloat16 [128, 128, 128], replicated, may hold values from -0.1875 to 0.1875
- coef_index: int32 [2048, 8], P('space'), may hold values from 0 to 127
- neighbours: int32 [2048, 7], P('space'), may hold values from 0 to 127
- send_lists: int32 [128, 16], P('space'), may hold values from -1 to 63, as said below
- mixing: float32 [16, 16], replicated, may hold values from -1.5 to 1.5
Outputs:
- finals: float32 [8, 16, 2048, 128], P('tm', None, 'space')
The draws below stay inside these ranges and needn't reach their ends.
Inputs may be any that keep to these rules, and one draw needn't show every extreme that they name: `send_lists`: in each row the live local block indices come first and -1 marks the empty slots after them; every row has 4 or more live slots; row 0 is full.
All inputs are finite; a program needn't handle non-finite values.
Results may differ from the reference program's by a relative error of at most 0.00065.
Values may be sent and summed in bfloat16 or wider, within the bound.
No kernel may reach another device: no remote copies, remote signals or barrier semaphores. Data moves between devices by JAX's collectives and lax.ppermute only.
A program may use at most 128 MiB of HBM per device.

```python
import math
import jax
import jax.numpy as jnp
from jax import lax

S = 16
CELLS = 128
NB = 64
HB = 16
TERMS = 8
NCOEF = 128
SWEEPS = 2
SLICES = 8
NBALL = 2048
LISTS = 128
N_SPACE = 32


def draw_send_lists(key, part):
    key = jax.random.fold_in(key, 11)
    count_key, index_key = jax.random.split(key)
    counts = jax.random.randint(count_key, (LISTS,), HB // 4, HB + 1)
    counts = counts.at[0].set(HB)
    blocks = jax.random.randint(index_key, (LISTS, HB), 0, NB)
    slots = jnp.arange(HB)
    return jnp.where(slots[None, :] < counts[:, None], blocks, -1).astype(jnp.int32)


def touch_ends(entries, key, least, top_value):
    longest = entries.shape.index(max(entries.shape))
    spots = []
    for shift in (0, 1):
        where = [jax.random.randint(jax.random.fold_in(key, axis), (), 0, length) for axis, length in enumerate(entries.shape)]
        where[longest] = (where[longest] + shift) % entries.shape[longest]
        spots.append(tuple(where))
    return entries.at[spots[0]].set(least).at[spots[1]].set(top_value)


def steps_of(stream_key, extent, pieces, smallest, top_value):
    factor_of, own = 1.0, jax.random.fold_in(stream_key, 6)
    for dim, blocks in pieces:
        steps = jnp.exp(jax.random.uniform(jax.random.fold_in(own, dim), (blocks,), jnp.float32, smallest / len(pieces), top_value / len(pieces)))
        factor_of = factor_of * jnp.repeat(steps, extent[dim] // blocks).reshape([-1 if axis == dim else 1 for axis in range(len(extent))])
    return factor_of


def centred(rng, shape, deviation, limit, shards=(), kind=jnp.bfloat16):
    array = deviation * jax.random.normal(rng, shape, jnp.float32)
    if shards:
        array = array * steps_of(rng, shape, shards, -0.22, 0.18)
    return jnp.clip(array, -limit, limit).astype(kind)


def setup_inputs(seed: int = 0) -> dict:
    seeds = jax.random.split(jax.random.key(seed), 7)
    return {
        "guess": centred(seeds[0], (SLICES, S, NBALL, CELLS), 1.0, 6.0, ((0, 8), (2, 32)), jnp.float32),
        "coeffs": centred(seeds[1], (NCOEF, CELLS, CELLS), (CELLS * TERMS) ** -0.5, 0.1875),
        "coef_index": touch_ends(jax.random.randint(seeds[2], (NBALL, TERMS), 0, NCOEF), jax.random.fold_in(seeds[2], 1), 0, NCOEF - 1).astype(jnp.int32),
        "neighbours": touch_ends(jax.random.randint(seeds[3], (NBALL, TERMS - 1), 0, NB + 4 * HB), jax.random.fold_in(seeds[3], 1), 0, (NB + 4 * HB) - 1).astype(jnp.int32),
        "send_lists": draw_send_lists(jax.random.fold_in(seeds[6], 71), 0),
        "mixing": centred(seeds[5], (S, S), S ** -0.5, 1.5, (), jnp.float32),
    }


step_size = 0.3
root_six = math.sqrt(6.0)
node_times = ((4.0 - root_six) / 10.0, (4.0 + root_six) / 10.0, 1.0)
radau_rows = (((88.0 - 7.0 * root_six) / 360.0, (296.0 - 169.0 * root_six) / 1800.0, (-2.0 + 3.0 * root_six) / 225.0), ((296.0 + 169.0 * root_six) / 1800.0, (88.0 + 7.0 * root_six) / 360.0, (-2.0 - 3.0 * root_six) / 225.0), ((16.0 - root_six) / 36.0, (16.0 + root_six) / 36.0, 1.0 / 9.0))
node_gaps = (node_times[0], node_times[1] - node_times[0], node_times[2] - node_times[1])
node_integrals = (radau_rows[0], tuple((radau_rows[1][j] - radau_rows[0][j] for j in range(3))), tuple((radau_rows[2][j] - radau_rows[1][j] for j in range(3))))

def shift_parts(packed, offset):
    width = abs(offset)
    zeros = jnp.zeros_like(packed[:, :, :width])
    if offset > 0:
        return jnp.concatenate([zeros, packed[:, :, :-width]], axis=2)
    return jnp.concatenate([packed[:, :, width:], zeros], axis=2)

def reference(guess, coeffs, coef_index, neighbours, send_lists, mixing):
    parts = N_SPACE
    slices = guess.shape[0]
    species = guess.shape[1]
    state_zero = guess.reshape(slices, species, parts, NB, CELLS)
    lists = send_lists.reshape(parts, 4 * HB)
    live = (lists >= 0).reshape(parts, 4, HB)
    safe = jnp.maximum(lists, 0).astype(jnp.int32)
    own_rows = jnp.broadcast_to(jnp.arange(NB, dtype=jnp.int32)[None, :, None], (parts, NB, 1))
    columns = jnp.concatenate([own_rows, neighbours.reshape(parts, NB, TERMS - 1).astype(jnp.int32)], axis=2)
    coef_parts = coef_index.reshape(parts, NB, TERMS)
    part_ids = jnp.arange(parts, dtype=jnp.int32)[:, None]

    def one_part(items):
        block_set, cols, cidx = items
        stack = coeffs[cidx].astype(jnp.float32)
        picked = block_set[:, :, cols, :].astype(jnp.float32)
        return jnp.einsum('nsbtc,btcd->nsbd', picked, stack, precision=lax.Precision.HIGHEST)

    def operate(field):
        rounded = field.astype(jnp.bfloat16)
        taken = rounded[:, :, part_ids, safe, :].reshape(slices, species, parts, 4, HB, CELLS)
        taken = jnp.where(live[None, None, :, :, :, None], taken, jnp.zeros((), jnp.bfloat16))
        received = [shift_parts(taken[:, :, :, slot], offset) for slot, offset in enumerate((1, -1, 2, -2))]
        extended = jnp.concatenate([rounded] + received, axis=3)
        moved = jnp.moveaxis(extended, 2, 0)
        linear = lax.map(one_part, (moved, columns, coef_parts))
        linear = jnp.moveaxis(linear, 0, 2)
        reaction = jnp.einsum('rs,nspbc->nrpbc', mixing, jnp.tanh(field), precision=lax.Precision.HIGHEST)
        return linear + reaction
    forces = [operate(state_zero)] * 4
    ending = state_zero
    for sweep in range(SWEEPS):
        start = jnp.concatenate([state_zero[:1], ending[:-1]], axis=0)
        f_current = operate(start)
        current = start
        new_forces = [f_current]
        for node in range(3):
            quad = node_integrals[node][0] * forces[1] + node_integrals[node][1] * forces[2] + node_integrals[node][2] * forces[3]
            current = current + step_size * (node_gaps[node] * (f_current - forces[node]) + quad)
            if node < 2 or sweep + 1 < SWEEPS:
                f_current = operate(current)
                new_forces.append(f_current)
        forces = new_forces
        ending = current
    return ending.reshape(slices, species, parts * NB, CELLS)
```

```python
import functools
import math

import jax
import jax.numpy as jnp
from jax import lax
from jax.experimental import pallas as pl
from jax.experimental.pallas import tpu as pltpu
from jax.sharding import PartitionSpec as P

SWEEPS = 2

step_size = 0.3
root_six = math.sqrt(6.0)
node_times = ((4.0 - root_six) / 10.0, (4.0 + root_six) / 10.0, 1.0)
radau_rows = (
    (
        (88.0 - 7.0 * root_six) / 360.0,
        (296.0 - 169.0 * root_six) / 1800.0,
        (-2.0 + 3.0 * root_six) / 225.0,
    ),
    (
        (296.0 + 169.0 * root_six) / 1800.0,
        (88.0 + 7.0 * root_six) / 360.0,
        (-2.0 - 3.0 * root_six) / 225.0,
    ),
    ((16.0 - root_six) / 36.0, (16.0 + root_six) / 36.0, 1.0 / 9.0),
)
node_gaps = (node_times[0], node_times[1] - node_times[0], node_times[2] - node_times[1])
node_integrals = (
    radau_rows[0],
    tuple((radau_rows[1][j] - radau_rows[0][j] for j in range(3))),
    tuple((radau_rows[2][j] - radau_rows[1][j] for j in range(3))),
)

f32 = jnp.float32
bf16 = jnp.bfloat16
VMEM = pl.BlockSpec(memory_space=pltpu.VMEM)
SMEM = pl.BlockSpec(memory_space=pltpu.SMEM)
PARAMS = pltpu.CompilerParams(vmem_limit_bytes=32 * 1024 * 1024)
UNROLL = 16


def pairing(slices, parts, distance, late):
    route = []
    for a in range(slices):
        for p in range(parts):
            ahead = ((p // distance) % 2 == 0) != late
            q = p + distance if ahead else p - distance
            b, q = (a, q) if 0 <= q < parts else (a ^ 1, p)
            route.append((a * parts + p, b * parts + q))
    return route


def swap(block, distance, late):
    route = pairing(lax.axis_size("tm"), lax.axis_size("space"), distance, late)
    return lax.ppermute(block, ("tm", "space"), route)


def next_slice(block):
    n = lax.axis_size("tm")
    return lax.ppermute(block, "tm", [(i, (i + 1) % n) for i in range(n)])


PAIRS = ((2, True), (2, False), (1, True), (1, False))


def exchange(packs):
    return tuple(swap(x, d, late) for x, (d, late) in zip(packs, PAIRS))


def plan():
    p = lax.axis_index("space")
    n = lax.axis_size("space")
    sends, fills, valid = [], [], []
    for distance, late in PAIRS:
        base = 0 if distance == 1 else 2
        ahead = ((p // distance) % 2 == 0) != late
        q = jnp.where(ahead, p + distance, p - distance)
        sends.append(jnp.where(ahead, base, base + 1))
        fills.append(jnp.where(ahead, base + 1, base))
        valid.append((q >= 0) & (q < n))
    leading = lax.axis_index("tm") == 0
    return jnp.stack([x.astype(jnp.int32) for x in sends + fills + valid + [leading]])


def pack(flags, lists, vb, packs):
    slots = packs[0].shape[0]
    for k, out in enumerate(packs):
        base = flags[k] * slots
        for j in range(slots):
            row = lists[base + j]
            block = vb[jnp.maximum(row, 0)]
            out[j] = jnp.where(row >= 0, block, jnp.zeros_like(block))


def first_kernel(flags, lists, u, vb, *packs):
    vb[...] = u[...].astype(bf16)
    pack(flags, lists, vb, packs)


def force_kernel(update, extras, keep, send, flags, lists, cols, cidx, u, vb, *refs):
    received, refs = refs[:4], refs[4:]
    coeffs, mix, refs = refs[0], refs[1], refs[2:]
    olds, refs = refs[:extras], refs[extras:]
    outs, ext = refs[:-1], refs[-1]
    nblocks = u.shape[0]
    slots = received[0].shape[0]
    terms = cols.shape[0] // nblocks
    ext[0:nblocks] = vb[...]
    for k, got in enumerate(received):
        live = flags[8 + k] > 0
        block = got[...]
        ext[pl.ds(nblocks + flags[4 + k] * slots, slots)] = jnp.where(live, block, jnp.zeros_like(block))
    mixv = mix[...]

    def body(i, carry):
        for j in range(UNROLL):
            b = i * UNROLL + j
            xs = [ext[cols[b * terms + t]] for t in range(terms)]
            ws = [coeffs[cidx[b * terms + t]] for t in range(terms)]
            field = u[b]
            th = jnp.tanh(field)
            hi = th.astype(bf16)
            lo = (th - hi.astype(f32)).astype(bf16)
            force = jnp.dot(
                jnp.concatenate(xs, axis=1), jnp.concatenate(ws, axis=0), preferred_element_type=f32
            )
            force += jnp.dot(mixv, jnp.concatenate([hi, hi, lo], axis=0), preferred_element_type=f32)
            at = 0
            if keep:
                outs[at][b] = force
                at += 1
            if update is None:
                outs[at][b] = force.astype(bf16)
                continue
            new = update(field, force, [old[b] for old in olds])
            outs[at][b] = new
            if send:
                outs[at + 1][b] = new.astype(bf16)
        return carry

    lax.fori_loop(0, nblocks // UNROLL, body, 0)
    if send:
        pack(flags, lists, outs[-5], outs[-4:])


def early_kernel(flags, lists, guess, incoming, force, moved, e0, u, vb, *packs):
    leading = flags[12] > 0
    g, q = node_gaps[0], sum(node_integrals[0])

    def body(b, carry):
        f = force[b]
        start = jnp.where(leading, guess[b], incoming[b])
        e = jnp.where(leading, f, moved[b].astype(f32))
        e0[b] = e
        new = start + step_size * (g * (e - f) + q * f)
        u[b] = new
        vb[b] = new.astype(bf16)
        return carry

    lax.fori_loop(0, u.shape[0], body, 0, unroll=8)
    pack(flags, lists, vb, packs)


def late_kernel(flags, lists, guess, incoming, moved, e0, e1, e2, e3, u, vb, *packs):
    leading = flags[12] > 0
    g, q = node_gaps[0], node_integrals[0]

    def body(b, carry):
        f = e0[b]
        start = jnp.where(leading, guess[b], incoming[b])
        e = jnp.where(leading, f, moved[b].astype(f32))
        quad = q[0] * e1[b] + q[1] * e2[b] + q[2] * e3[b]
        new = start + step_size * (g * (e - f) + quad)
        u[b] = new
        vb[b] = new.astype(bf16)
        return carry

    lax.fori_loop(0, u.shape[0], body, 0, unroll=8)
    pack(flags, lists, vb, packs)


def node_update_first(node):
    g, q = node_gaps[node], sum(node_integrals[node])

    def update(u, e, olds):
        (f,) = olds
        return u + step_size * (g * (e - f) + q * f)

    return update


def node_update_second(node):
    g, q = node_gaps[node], node_integrals[node]

    def update(u, e, olds):
        quad = q[0] * olds[0] + q[1] * olds[1] + q[2] * olds[2]
        return u + step_size * (g * (e - olds[node - 1]) + quad)

    return update


def per_device(guess, coeffs, coef_index, neighbours, send_lists, mixing):
    first = jnp.transpose(guess[0], (1, 0, 2))
    nblocks, species, cells = first.shape
    slots = send_lists.shape[1]
    own_rows = lax.broadcasted_iota(jnp.int32, (nblocks, 1), 0)
    cols = jnp.concatenate([own_rows, neighbours], axis=1).reshape(-1)
    cidx = coef_index.reshape(-1)
    lists = send_lists.reshape(-1)
    flags = plan()
    mix_hi = mixing.astype(bf16)
    mix_lo = (mixing - mix_hi.astype(f32)).astype(bf16)
    mix = jnp.concatenate([mix_hi, mix_lo, mix_hi], axis=1)

    state = jax.ShapeDtypeStruct((nblocks, species, cells), f32)
    rounded = jax.ShapeDtypeStruct((nblocks, species, cells), bf16)
    rim = jax.ShapeDtypeStruct((slots, species, cells), bf16)

    def call(kernel, outs, scalars, arrays, scratch=()):
        return pl.pallas_call(
            kernel,
            out_shape=outs,
            in_specs=[SMEM] * len(scalars) + [VMEM] * len(arrays),
            out_specs=[VMEM] * len(outs),
            scratch_shapes=scratch,
            compiler_params=PARAMS,
        )(*scalars, *arrays)

    ext = [pltpu.VMEM((nblocks + 4 * slots, species, cells), bf16)]

    def force(u, vb, received, update, olds, keep, send):
        outs = []
        if keep:
            outs.append(state)
        if update is None:
            outs.append(rounded)
        else:
            outs.append(state)
        if send:
            outs += [rounded] + [rim] * 4
        kernel = functools.partial(force_kernel, update, len(olds), keep, send)
        return call(
            kernel, outs, (flags, lists, cols, cidx), (u, vb, *received, coeffs, mix, *olds), ext
        )

    vb, *packs = call(first_kernel, [rounded] + [rim] * 4, (flags, lists), (first,))
    received = exchange(packs)
    came = next_slice(first)
    f, fb = force(first, vb, received, None, (), True, False)
    e0, u, vb, *packs = call(
        early_kernel,
        [state, state, rounded] + [rim] * 4,
        (flags, lists),
        (first, came, f, next_slice(fb)),
    )
    e1, u, vb, *packs = force(u, vb, exchange(packs), node_update_first(1), (f,), True, True)
    e2, u, vb, *packs = force(u, vb, exchange(packs), node_update_first(2), (f,), True, True)
    received = exchange(packs)
    came = next_slice(u)
    e3, e3b = force(u, vb, received, None, (), True, False)
    u, vb, *packs = call(
        late_kernel,
        [state, rounded] + [rim] * 4,
        (flags, lists),
        (first, came, next_slice(e3b), e0, e1, e2, e3),
    )
    olds = (e1, e2, e3)
    u, vb, *packs = force(u, vb, exchange(packs), node_update_second(1), olds, False, True)
    (end,) = force(u, vb, exchange(packs), node_update_second(2), olds, False, False)
    return jnp.transpose(end, (1, 0, 2))[None]


def solution(mesh):
    placed = (
        P("tm", None, "space", None),
        P(),
        P("space", None),
        P("space", None),
        P("space", None),
        P(),
    )
    return jax.shard_map(
        per_device,
        mesh=mesh,
        in_specs=placed,
        out_specs=P("tm", None, "space", None),
        check_vma=False,
    )
```

```python
import functools
import math

import jax
import jax.numpy as jnp
from jax import lax
from jax.experimental import pallas as pl
from jax.experimental.pallas import tpu as pltpu
from jax.sharding import PartitionSpec as P

SWEEPS = 2

step_size = 0.3
root_six = math.sqrt(6.0)
node_times = ((4.0 - root_six) / 10.0, (4.0 + root_six) / 10.0, 1.0)
radau_rows = (
    (
        (88.0 - 7.0 * root_six) / 360.0,
        (296.0 - 169.0 * root_six) / 1800.0,
        (-2.0 + 3.0 * root_six) / 225.0,
    ),
    (
        (296.0 + 169.0 * root_six) / 1800.0,
        (88.0 + 7.0 * root_six) / 360.0,
        (-2.0 - 3.0 * root_six) / 225.0,
    ),
    ((16.0 - root_six) / 36.0, (16.0 + root_six) / 36.0, 1.0 / 9.0),
)
node_gaps = (node_times[0], node_times[1] - node_times[0], node_times[2] - node_times[1])
node_integrals = (
    radau_rows[0],
    tuple((radau_rows[1][j] - radau_rows[0][j] for j in range(3))),
    tuple((radau_rows[2][j] - radau_rows[1][j] for j in range(3))),
)

f32 = jnp.float32
bf16 = jnp.bfloat16
VMEM = pl.BlockSpec(memory_space=pltpu.VMEM)
SMEM = pl.BlockSpec(memory_space=pltpu.SMEM)
PARAMS = pltpu.CompilerParams(vmem_limit_bytes=32 * 1024 * 1024)
UNROLL = 16


def pairing(slices, parts, distance, late):
    route = []
    for a in range(slices):
        for p in range(parts):
            ahead = ((p // distance) % 2 == 0) != late
            q = p + distance if ahead else p - distance
            b, q = (a, q) if 0 <= q < parts else (a ^ 1, p)
            route.append((a * parts + p, b * parts + q))
    return route


def swap(block, distance, late):
    route = pairing(lax.axis_size("tm"), lax.axis_size("space"), distance, late)
    return lax.ppermute(block, ("tm", "space"), route)


def next_slice(block):
    n = lax.axis_size("tm")
    return lax.ppermute(block, "tm", [(i, (i + 1) % n) for i in range(n)])


PAIRS = ((2, True), (2, False), (1, True), (1, False))


def exchange(packs):
    return tuple(swap(x, d, late) for x, (d, late) in zip(packs, PAIRS))


def plan():
    p = lax.axis_index("space")
    n = lax.axis_size("space")
    sends, fills, valid = [], [], []
    for distance, late in PAIRS:
        base = 0 if distance == 1 else 2
        ahead = ((p // distance) % 2 == 0) != late
        q = jnp.where(ahead, p + distance, p - distance)
        sends.append(jnp.where(ahead, base, base + 1))
        fills.append(jnp.where(ahead, base + 1, base))
        valid.append((q >= 0) & (q < n))
    leading = lax.axis_index("tm") == 0
    return jnp.stack([x.astype(jnp.int32) for x in sends + fills + valid + [leading]])


def pack(flags, lists, vb, packs):
    slots = packs[0].shape[0]
    for k, out in enumerate(packs):
        for j in range(slots):
            row = lists[flags[k], j]
            block = vb[jnp.maximum(row, 0)]
            out[j] = jnp.where(row >= 0, block, jnp.zeros_like(block))


def first_kernel(flags, lists, u, vb, *packs):
    vb[...] = u[...].astype(bf16)
    pack(flags, lists, vb, packs)


def own_kernel(cidx, u, vb, coeffs, mixing, part):
    m = mixing[...]
    m_hi = m.astype(bf16)
    m_lo = (m - m_hi.astype(f32)).astype(bf16)
    mix = jnp.concatenate([m_hi, m_lo, m_hi], axis=1)

    def body(i, carry):
        for j in range(UNROLL):
            b = i * UNROLL + j
            th = jnp.tanh(u[b])
            hi = th.astype(bf16)
            lo = (th - hi.astype(f32)).astype(bf16)
            own = jnp.dot(vb[b], coeffs[cidx[b, 0]], preferred_element_type=f32)
            part[b] = own + jnp.dot(mix, jnp.concatenate([hi, hi, lo], axis=0), preferred_element_type=f32)
        return carry

    lax.fori_loop(0, u.shape[0] // UNROLL, body, 0)


def force_kernel(update, extras, keep, send, flags, lists, cols, cidx, u, vb, part, *refs):
    received, refs = refs[:4], refs[4:]
    coeffs, refs = refs[0], refs[1:]
    olds, refs = refs[:extras], refs[extras:]
    outs, ext = refs[:-1], refs[-1]
    nblocks = vb.shape[0]
    slots = received[0].shape[0]
    terms = cols.shape[1]
    ext[0:nblocks] = vb[...]
    for k, got in enumerate(received):
        live = flags[8 + k] > 0
        block = got[...]
        ext[pl.ds(nblocks + flags[4 + k] * slots, slots)] = jnp.where(live, block, jnp.zeros_like(block))

    def body(i, carry):
        for j in range(UNROLL):
            b = i * UNROLL + j
            xs = [ext[cols[b, t]] for t in range(terms)]
            ws = [coeffs[cidx[b, t + 1]] for t in range(terms)]
            force = part[b] + jnp.dot(
                jnp.concatenate(xs, axis=1), jnp.concatenate(ws, axis=0), preferred_element_type=f32
            )
            at = 0
            if keep:
                outs[at][b] = force
                at += 1
            if update is None:
                outs[at][b] = force.astype(bf16)
                continue
            new = update(u[b], force, [old[b] for old in olds])
            outs[at][b] = new
            if send:
                outs[at + 1][b] = new.astype(bf16)
        return carry

    lax.fori_loop(0, nblocks // UNROLL, body, 0)
    if send:
        pack(flags, lists, outs[-5], outs[-4:])


def early_kernel(flags, lists, guess, incoming, force, moved, e0, u, vb, *packs):
    leading = flags[12] > 0
    g, q = node_gaps[0], sum(node_integrals[0])

    def body(b, carry):
        f = force[b]
        start = jnp.where(leading, guess[b], incoming[b])
        e = jnp.where(leading, f, moved[b].astype(f32))
        e0[b] = e
        new = start + step_size * (g * (e - f) + q * f)
        u[b] = new
        vb[b] = new.astype(bf16)
        return carry

    lax.fori_loop(0, u.shape[0], body, 0, unroll=8)
    pack(flags, lists, vb, packs)


def late_kernel(flags, lists, guess, incoming, moved, e0, e1, e2, e3, u, vb, *packs):
    leading = flags[12] > 0
    g, q = node_gaps[0], node_integrals[0]

    def body(b, carry):
        f = e0[b]
        start = jnp.where(leading, guess[b], incoming[b])
        e = jnp.where(leading, f, moved[b].astype(f32))
        quad = q[0] * e1[b] + q[1] * e2[b] + q[2] * e3[b]
        new = start + step_size * (g * (e - f) + quad)
        u[b] = new
        vb[b] = new.astype(bf16)
        return carry

    lax.fori_loop(0, u.shape[0], body, 0, unroll=8)
    pack(flags, lists, vb, packs)


def node_update_first(node):
    g, q = node_gaps[node], sum(node_integrals[node])

    def update(u, e, olds):
        (f,) = olds
        return u + step_size * (g * (e - f) + q * f)

    return update


def node_update_second(node):
    g, q = node_gaps[node], node_integrals[node]

    def update(u, e, olds):
        quad = q[0] * olds[0] + q[1] * olds[1] + q[2] * olds[2]
        return u + step_size * (g * (e - olds[node - 1]) + quad)

    return update


def per_device(guess, coeffs, coef_index, neighbours, send_lists, mixing):
    first = jnp.transpose(guess[0], (1, 0, 2))
    nblocks, species, cells = first.shape
    slots = send_lists.shape[1]
    lists = send_lists
    flags = plan()

    state = jax.ShapeDtypeStruct((nblocks, species, cells), f32)
    rounded = jax.ShapeDtypeStruct((nblocks, species, cells), bf16)
    rim = jax.ShapeDtypeStruct((slots, species, cells), bf16)

    def call(kernel, outs, scalars, arrays, scratch=(), cost=4_000_000):
        return pl.pallas_call(
            kernel,
            out_shape=outs,
            in_specs=[SMEM] * len(scalars) + [VMEM] * len(arrays),
            out_specs=[VMEM] * len(outs),
            scratch_shapes=scratch,
            compiler_params=PARAMS,
            cost_estimate=pl.CostEstimate(flops=cost, bytes_accessed=cost, transcendentals=0),
        )(*scalars, *arrays)

    ext = [pltpu.VMEM((nblocks + 4 * slots, species, cells), bf16)]

    def force(u, vb, received, update, olds, keep, send):
        (part,) = call(own_kernel, [state], (coef_index,), (u, vb, coeffs, mixing))
        outs = []
        if keep:
            outs.append(state)
        if update is None:
            outs.append(rounded)
        else:
            outs.append(state)
        if send:
            outs += [rounded] + [rim] * 4
        kernel = functools.partial(force_kernel, update, len(olds), keep, send)
        return call(
            kernel,
            outs,
            (flags, lists, neighbours, coef_index),
            (u, vb, part, *received, coeffs, *olds),
            ext,
        )

    vb, *packs = call(first_kernel, [rounded] + [rim] * 4, (flags, lists), (first,))
    received = exchange(packs)
    came = next_slice(first)
    f, fb = force(first, vb, received, None, (), True, False)
    e0, u, vb, *packs = call(
        early_kernel,
        [state, state, rounded] + [rim] * 4,
        (flags, lists),
        (first, came, f, next_slice(fb)),
    )
    e1, u, vb, *packs = force(u, vb, exchange(packs), node_update_first(1), (f,), True, True)
    e2, u, vb, *packs = force(u, vb, exchange(packs), node_update_first(2), (f,), True, True)
    received = exchange(packs)
    came = next_slice(u)
    e3, e3b = force(u, vb, received, None, (), True, False)
    u, vb, *packs = call(
        late_kernel,
        [state, rounded] + [rim] * 4,
        (flags, lists),
        (first, came, next_slice(e3b), e0, e1, e2, e3),
    )
    olds = (e1, e2, e3)
    u, vb, *packs = force(u, vb, exchange(packs), node_update_second(1), olds, False, True)
    (end,) = force(u, vb, exchange(packs), node_update_second(2), olds, False, False)
    return jnp.transpose(end, (1, 0, 2))[None]


def solution(mesh):
    placed = (
        P("tm", None, "space", None),
        P(),
        P("space", None),
        P("space", None),
        P("space", None),
        P(),
    )
    return jax.shard_map(
        per_device,
        mesh=mesh,
        in_specs=placed,
        out_specs=P("tm", None, "space", None),
        check_vma=False,
    )
```

```python
import functools
import math

import jax
import jax.numpy as jnp
from jax import lax
from jax.experimental import pallas as pl
from jax.experimental.pallas import tpu as pltpu
from jax.sharding import PartitionSpec as P

SWEEPS = 2

step_size = 0.3
root_six = math.sqrt(6.0)
node_times = ((4.0 - root_six) / 10.0, (4.0 + root_six) / 10.0, 1.0)
radau_rows = (
    (
        (88.0 - 7.0 * root_six) / 360.0,
        (296.0 - 169.0 * root_six) / 1800.0,
        (-2.0 + 3.0 * root_six) / 225.0,
    ),
    (
        (296.0 + 169.0 * root_six) / 1800.0,
        (88.0 + 7.0 * root_six) / 360.0,
        (-2.0 - 3.0 * root_six) / 225.0,
    ),
    ((16.0 - root_six) / 36.0, (16.0 + root_six) / 36.0, 1.0 / 9.0),
)
node_gaps = (node_times[0], node_times[1] - node_times[0], node_times[2] - node_times[1])
node_integrals = (
    radau_rows[0],
    tuple((radau_rows[1][j] - radau_rows[0][j] for j in range(3))),
    tuple((radau_rows[2][j] - radau_rows[1][j] for j in range(3))),
)

f32 = jnp.float32
bf16 = jnp.bfloat16
VMEM = pl.BlockSpec(memory_space=pltpu.VMEM)
SMEM = pl.BlockSpec(memory_space=pltpu.SMEM)
PARAMS = pltpu.CompilerParams(vmem_limit_bytes=8 * 1024 * 1024)
UNROLL = 16


def pairing(slices, parts, distance, late):
    route = []
    for a in range(slices):
        for p in range(parts):
            ahead = ((p // distance) % 2 == 0) != late
            q = p + distance if ahead else p - distance
            b, q = (a, q) if 0 <= q < parts else (a ^ 1, p)
            route.append((a * parts + p, b * parts + q))
    return route


def swap(block, distance, late):
    route = pairing(lax.axis_size("tm"), lax.axis_size("space"), distance, late)
    return lax.ppermute(block, ("tm", "space"), route)


def next_slice(block):
    n = lax.axis_size("tm")
    return lax.ppermute(block, "tm", [(i, (i + 1) % n) for i in range(n)])


PLAN = 13
PAIRS = ((2, True), (2, False), (1, True), (1, False))


def exchange(packs):
    return tuple(swap(x, d, late) for x, (d, late) in zip(packs, PAIRS))


def plan():
    p = lax.axis_index("space")
    n = lax.axis_size("space")
    sends, fills, valid = [], [], []
    for distance, late in PAIRS:
        base = 0 if distance == 1 else 2
        ahead = ((p // distance) % 2 == 0) != late
        q = jnp.where(ahead, p + distance, p - distance)
        sends.append(jnp.where(ahead, base, base + 1))
        fills.append(jnp.where(ahead, base + 1, base))
        valid.append((q >= 0) & (q < n))
    leading = lax.axis_index("tm") == 0
    return jnp.stack([x.astype(jnp.int32) for x in sends + fills + valid + [leading]])


def pack(flags, vb, packs):
    slots = packs[0].shape[0]
    for k, out in enumerate(packs):
        first = PLAN + flags[k] * slots
        for j in range(slots):
            row = flags[first + j]
            block = vb[jnp.maximum(row, 0)]
            out[j] = jnp.where(row >= 0, block, jnp.zeros_like(block))


def first_kernel(flags, u, vb, *packs):
    vb[...] = u[...].astype(bf16)
    pack(flags, vb, packs)


def first_reaction_kernel(u, mixing, coeffs, part, mix):
    del coeffs
    m = mixing[...]
    m_hi = m.astype(bf16)
    m_lo = (m - m_hi.astype(f32)).astype(bf16)
    mix[...] = jnp.concatenate([m_hi, m_lo, m_hi], axis=1)
    reaction_kernel(None, 0, u, mix, part)


def reaction_kernel(prepare, extras, u, mix, *refs):
    olds, outs = refs[:extras], refs[extras:]
    mixv = mix[...]

    def body(i, carry):
        for j in range(UNROLL):
            b = i * UNROLL + j
            field = u[b]
            th = jnp.tanh(field)
            hi = th.astype(bf16)
            lo = (th - hi.astype(f32)).astype(bf16)
            outs[0][b] = jnp.dot(mixv, jnp.concatenate([hi, hi, lo], axis=0), preferred_element_type=f32)
            if prepare is not None:
                outs[1][b] = prepare(field, [old[b] for old in olds])
        return carry

    lax.fori_loop(0, u.shape[0] // UNROLL, body, 0)


def force_kernel(gap, keep, send, flags, table, vb, part, *refs):
    received, refs = refs[:4], refs[4:]
    coeffs, refs = refs[0], refs[1:]
    if gap is not None:
        base, refs = refs[0], refs[1:]
    outs, ext = refs[:-1], refs[-1]
    nblocks = vb.shape[0]
    slots = received[0].shape[0]
    width = table.shape[0] // nblocks
    terms = (width + 1) // 2
    ext[0:nblocks] = vb[...]
    for k, got in enumerate(received):
        live = flags[8 + k] > 0
        block = got[...]
        ext[pl.ds(nblocks + flags[4 + k] * slots, slots)] = jnp.where(live, block, jnp.zeros_like(block))

    def body(i, carry):
        for j in range(UNROLL):
            b = i * UNROLL + j
            xs = [vb[b]] + [ext[table[b * width + terms + t]] for t in range(terms - 1)]
            ws = [coeffs[table[b * width + t]] for t in range(terms)]
            force = part[b] + jnp.dot(
                jnp.concatenate(xs, axis=1), jnp.concatenate(ws, axis=0), preferred_element_type=f32
            )
            at = 0
            if keep:
                outs[at][b] = force
                at += 1
            if gap is None:
                outs[at][b] = force.astype(bf16)
                continue
            new = base[b] + (step_size * gap) * force
            outs[at][b] = new
            if send:
                outs[at + 1][b] = new.astype(bf16)
        return carry

    lax.fori_loop(0, nblocks // UNROLL, body, 0)
    if send:
        pack(flags, outs[-5], outs[-4:])


def early_kernel(flags, guess, incoming, force, moved, e0, u, vb, *packs):
    leading = flags[12] > 0
    g, q = node_gaps[0], sum(node_integrals[0])

    def body(b, carry):
        f = force[b]
        start = jnp.where(leading, guess[b], incoming[b])
        e = jnp.where(leading, f, moved[b].astype(f32))
        e0[b] = e
        new = start + step_size * (g * (e - f) + q * f)
        u[b] = new
        vb[b] = new.astype(bf16)
        return carry

    lax.fori_loop(0, u.shape[0], body, 0, unroll=8)
    pack(flags, vb, packs)


def late_kernel(flags, guess, incoming, moved, e0, e1, e2, e3, u, vb, *packs):
    leading = flags[12] > 0
    g, q = node_gaps[0], node_integrals[0]

    def body(b, carry):
        f = e0[b]
        start = jnp.where(leading, guess[b], incoming[b])
        e = jnp.where(leading, f, moved[b].astype(f32))
        quad = q[0] * e1[b] + q[1] * e2[b] + q[2] * e3[b]
        new = start + step_size * (g * (e - f) + quad)
        u[b] = new
        vb[b] = new.astype(bf16)
        return carry

    lax.fori_loop(0, u.shape[0], body, 0, unroll=8)
    pack(flags, vb, packs)


def prepare_first(node):
    g, q = node_gaps[node], sum(node_integrals[node])

    def prepare(u, olds):
        (f,) = olds
        return u + step_size * (q * f - g * f)

    return prepare


def prepare_second(node):
    g, q = node_gaps[node], node_integrals[node]

    def prepare(u, olds):
        quad = q[0] * olds[0] + q[1] * olds[1] + q[2] * olds[2]
        return u + step_size * (quad - g * olds[node - 1])

    return prepare


def per_device(guess, coeffs, coef_index, neighbours, send_lists, mixing):
    first = jnp.transpose(guess[0], (1, 0, 2))
    nblocks, species, cells = first.shape
    slots = send_lists.shape[1]
    flags = jnp.concatenate([plan(), send_lists.reshape(-1)])
    table = jnp.concatenate([coef_index, neighbours], axis=1).reshape(-1)

    state = jax.ShapeDtypeStruct((nblocks, species, cells), f32)
    rounded = jax.ShapeDtypeStruct((nblocks, species, cells), bf16)
    rim = jax.ShapeDtypeStruct((slots, species, cells), bf16)

    def call(kernel, outs, scalars, arrays, scratch=(), cost=4_000_000):
        return pl.pallas_call(
            kernel,
            out_shape=outs,
            in_specs=[SMEM] * len(scalars) + [VMEM] * len(arrays),
            out_specs=[VMEM] * len(outs),
            scratch_shapes=scratch,
            compiler_params=PARAMS,
            cost_estimate=pl.CostEstimate(flops=cost, bytes_accessed=cost, transcendentals=0),
        )(*scalars, *arrays)

    ext = [pltpu.VMEM((nblocks + 4 * slots, species, cells), bf16)]
    vb, *packs = call(first_kernel, [rounded] + [rim] * 4, (flags,), (first,))

    part, mix = call(
        first_reaction_kernel,
        [state, jax.ShapeDtypeStruct((species, 3 * species), bf16)],
        (),
        (first, mixing, coeffs),
    )

    def force(u, vb, packs, node, prepare, olds, keep, send, part=None):
        received = exchange(packs)
        rest = ()
        if part is None:
            kernel = functools.partial(reaction_kernel, prepare, len(olds))
            outs = [state] * (1 + (prepare is not None))
            part, *rest = call(kernel, outs, (), (u, mix, *olds))
        outs = [state] * keep + [rounded if node is None else state]
        if send:
            outs += [rounded] + [rim] * 4
        gap = None if node is None else node_gaps[node]
        kernel = functools.partial(force_kernel, gap, keep, send)
        return call(kernel, outs, (flags, table), (vb, part, *received, coeffs, *rest), ext)

    f, fb = force(first, vb, packs, None, None, (), True, False, part)
    e0, u, vb, *packs = call(
        early_kernel,
        [state, state, rounded] + [rim] * 4,
        (flags,),
        (first, next_slice(first), f, next_slice(fb)),
    )
    e1, u, vb, *packs = force(u, vb, packs, 1, prepare_first(1), (f,), True, True)
    e2, u, vb, *packs = force(u, vb, packs, 2, prepare_first(2), (f,), True, True)
    came = next_slice(u)
    e3, e3b = force(u, vb, packs, None, None, (), True, False)
    u, vb, *packs = call(
        late_kernel,
        [state, rounded] + [rim] * 4,
        (flags,),
        (first, came, next_slice(e3b), e0, e1, e2, e3),
    )
    olds = (e1, e2, e3)
    u, vb, *packs = force(u, vb, packs, 1, prepare_second(1), olds, False, True)
    (end,) = force(u, vb, packs, 2, prepare_second(2), olds, False, False)
    return jnp.transpose(end, (1, 0, 2))[None]


def solution(mesh):
    placed = (
        P("tm", None, "space", None),
        P(),
        P("space", None),
        P("space", None),
        P("space", None),
        P(),
    )
    return jax.shard_map(
        per_device,
        mesh=mesh,
        in_specs=placed,
        out_specs=P("tm", None, "space", None),
        check_vma=False,
    )
```

```python
import functools
import math

import jax
import jax.numpy as jnp
from jax import lax
from jax.experimental import pallas as pl
from jax.experimental.pallas import tpu as pltpu
from jax.sharding import PartitionSpec as P

SWEEPS = 2

step_size = 0.3
root_six = math.sqrt(6.0)
node_times = ((4.0 - root_six) / 10.0, (4.0 + root_six) / 10.0, 1.0)
radau_rows = (
    (
        (88.0 - 7.0 * root_six) / 360.0,
        (296.0 - 169.0 * root_six) / 1800.0,
        (-2.0 + 3.0 * root_six) / 225.0,
    ),
    (
        (296.0 + 169.0 * root_six) / 1800.0,
        (88.0 + 7.0 * root_six) / 360.0,
        (-2.0 - 3.0 * root_six) / 225.0,
    ),
    ((16.0 - root_six) / 36.0, (16.0 + root_six) / 36.0, 1.0 / 9.0),
)
node_gaps = (node_times[0], node_times[1] - node_times[0], node_times[2] - node_times[1])
node_integrals = (
    radau_rows[0],
    tuple((radau_rows[1][j] - radau_rows[0][j] for j in range(3))),
    tuple((radau_rows[2][j] - radau_rows[1][j] for j in range(3))),
)

f32 = jnp.float32
bf16 = jnp.bfloat16
VMEM = pl.BlockSpec(memory_space=pltpu.VMEM)
SMEM = pl.BlockSpec(memory_space=pltpu.SMEM)
PARAMS = pltpu.CompilerParams(vmem_limit_bytes=8 * 1024 * 1024)
UNROLL = 32


def pairing(slices, parts, distance, late):
    route = []
    for a in range(slices):
        for p in range(parts):
            ahead = ((p // distance) % 2 == 0) != late
            q = p + distance if ahead else p - distance
            b, q = (a, q) if 0 <= q < parts else (a ^ 1, p)
            route.append((a * parts + p, b * parts + q))
    return route


def swap(block, distance, late):
    route = pairing(lax.axis_size("tm"), lax.axis_size("space"), distance, late)
    return lax.ppermute(block, ("tm", "space"), route)


def next_slice(block):
    n = lax.axis_size("tm")
    return lax.ppermute(block, "tm", [(i, (i + 1) % n) for i in range(n)])


PLAN = 13
PAIRS = ((2, True), (2, False), (1, True), (1, False))


def exchange(packs):
    return tuple(swap(x, d, late) for x, (d, late) in zip(packs, PAIRS))


def plan():
    p = lax.axis_index("space")
    n = lax.axis_size("space")
    sends, fills, valid = [], [], []
    for distance, late in PAIRS:
        base = 0 if distance == 1 else 2
        ahead = ((p // distance) % 2 == 0) != late
        q = jnp.where(ahead, p + distance, p - distance)
        sends.append(jnp.where(ahead, base, base + 1))
        fills.append(jnp.where(ahead, base + 1, base))
        valid.append((q >= 0) & (q < n))
    leading = lax.axis_index("tm") == 0
    return jnp.stack([x.astype(jnp.int32) for x in sends + fills + valid + [leading]])


def pack(flags, vb, packs):
    slots = packs[0].shape[0]
    for k, out in enumerate(packs):
        first = PLAN + flags[k] * slots
        for j in range(slots):
            out[j] = vb[flags[first + j]]


def first_kernel(flags, u, vb, *packs):
    nblocks = u.shape[0]
    vb[0:nblocks] = u[...].astype(bf16)
    vb[nblocks] = jnp.zeros(vb.shape[1:], bf16)
    pack(flags, vb, packs)


def react(mix, field):
    th = jnp.tanh(field)
    hi = th.astype(bf16)
    lo = (th - hi.astype(f32)).astype(bf16)
    return jnp.dot(mix, jnp.concatenate([hi, hi, lo], axis=0), preferred_element_type=f32)


def per_block(count, body):
    def several(i, carry):
        for j in range(UNROLL):
            body(i * UNROLL + j)
        return carry

    lax.fori_loop(0, count // UNROLL, several, 0)


def first_reaction_kernel(u, mixing, coeffs, part, mix):
    del coeffs
    m = mixing[...]
    m_hi = m.astype(bf16)
    m_lo = (m - m_hi.astype(f32)).astype(bf16)
    mix[...] = jnp.concatenate([m_hi, m_lo, m_hi], axis=1)
    mixv = mix[...]

    def body(b):
        part[b] = react(mixv, u[b])

    per_block(u.shape[0], body)


def reaction_kernel(prepare, extras, u, mix, *refs):
    olds, (part, base) = refs[:extras], refs[extras:]
    mixv = mix[...]

    def body(b):
        field = u[b]
        part[b] = react(mixv, field)
        base[b] = prepare(field, [old[b] for old in olds])

    per_block(u.shape[0], body)


def moved_pack_kernel(step, extras, flags, *refs):
    arrays, packs = refs[:extras], refs[extras:]
    nblocks = arrays[0].shape[0]
    slots = packs[0].shape[0]
    leading = flags[PLAN - 1] > 0
    for k, out in enumerate(packs):
        first = PLAN + flags[k] * slots
        for j in range(slots):
            row = flags[first + j]
            block = step(leading, arrays, jnp.minimum(row, nblocks - 1))[0].astype(bf16)
            out[j] = jnp.where(row < nblocks, block, jnp.zeros_like(block))


def moved_reaction_kernel(step, prepare, extras, inputs, keep, flags, mix, *refs):
    arrays, olds, outs = refs[:extras], refs[extras:inputs], refs[inputs:]
    part, base, vb = outs[:3]
    nblocks = part.shape[0]
    leading = flags[PLAN - 1] > 0
    mixv = mix[...]
    vb[nblocks] = jnp.zeros(vb.shape[1:], bf16)

    def body(b):
        field, force = step(leading, arrays, b)
        if keep:
            outs[3][b] = force
        vb[b] = field.astype(bf16)
        part[b] = react(mixv, field)
        base[b] = prepare(field, [old[b] for old in olds])

    per_block(nblocks, body)


def force_kernel(weight, keep, shift, send, flags, table, vb, part, *refs):
    received, refs = refs[:4], refs[4:]
    coeffs, refs = refs[0], refs[1:]
    if weight is not None:
        base, refs = refs[0], refs[1:]
    outs, ext = list(refs[:-1]), refs[-1]
    forces = outs.pop(0) if keep else None
    shifted = outs.pop(0) if shift else None
    states = outs.pop(0) if weight is not None else None
    rounded = outs.pop(0) if send else None
    nblocks = part.shape[0]
    slots = received[0].shape[0]
    width = table.shape[0] // nblocks
    terms = (width + 1) // 2
    ext[0:nblocks] = vb[0:nblocks]
    for k, got in enumerate(received):
        live = flags[8 + k] > 0
        block = got[...]
        ext[pl.ds(nblocks + flags[4 + k] * slots, slots)] = jnp.where(live, block, jnp.zeros_like(block))

    def body(b):
        xs = [vb[b]] + [ext[table[b * width + terms + t]] for t in range(terms - 1)]
        ws = [coeffs[table[b * width + t]] for t in range(terms)]
        force = part[b] + jnp.dot(
            jnp.concatenate(xs, axis=1), jnp.concatenate(ws, axis=0), preferred_element_type=f32
        )
        if keep:
            forces[b] = force
        if shift:
            shifted[b] = force.astype(bf16)
        if weight is not None:
            new = base[b] + weight * force
            states[b] = new
            if send:
                rounded[b] = new.astype(bf16)

    per_block(nblocks, body)
    if send:
        rounded[nblocks] = jnp.zeros(rounded.shape[1:], bf16)
        pack(flags, rounded, outs)


def early_step(leading, arrays, b):
    guess, incoming, force, moved = arrays
    g, q = node_gaps[0], sum(node_integrals[0])
    f = force[b]
    start = jnp.where(leading, guess[b], incoming[b])
    e = jnp.where(leading, f, moved[b].astype(f32))
    return start + step_size * (g * (e - f) + q * f), e


def late_step(leading, arrays, b):
    guess, incoming, force, moved, olds = arrays
    start = jnp.where(leading, guess[b], incoming[b])
    e = jnp.where(leading, force[b], moved[b].astype(f32))
    return start + olds[b] + (step_size * node_gaps[0]) * e, e


def prepare_first(node):
    g, q = node_gaps[node], sum(node_integrals[node])

    def prepare(u, olds):
        (f,) = olds
        return u + step_size * (q * f - g * f)

    return prepare


def prepare_second(node):
    g, q = node_gaps[node], node_integrals[node]

    def prepare(u, olds):
        quad = q[0] * olds[0] + q[1] * olds[1] + q[2] * olds[2]
        return u + step_size * (quad - g * olds[node - 1])

    return prepare


def prepare_late(u, olds):
    e0, e1, e2 = olds
    q = node_integrals[0]
    return step_size * (q[0] * e1 + q[1] * e2 - node_gaps[0] * e0)


def per_device(guess, coeffs, coef_index, neighbours, send_lists, mixing):
    first = jnp.transpose(guess[0], (1, 0, 2))
    nblocks, species, cells = first.shape
    slots = send_lists.shape[1]
    rows = jnp.where(send_lists < 0, nblocks, send_lists)
    flags = jnp.concatenate([plan(), rows.reshape(-1)])
    table = jnp.concatenate([coef_index, neighbours], axis=1).reshape(-1)

    state = jax.ShapeDtypeStruct((nblocks, species, cells), f32)
    shifted = jax.ShapeDtypeStruct((nblocks, species, cells), bf16)
    rounded = jax.ShapeDtypeStruct((nblocks + 1, species, cells), bf16)
    rims = [jax.ShapeDtypeStruct((slots, species, cells), bf16)] * 4
    ext = [pltpu.VMEM((nblocks + 4 * slots, species, cells), bf16)]

    def call(kernel, outs, scalars, arrays, scratch=(), cost=4_000_000):
        return pl.pallas_call(
            kernel,
            out_shape=outs,
            in_specs=[SMEM] * len(scalars) + [VMEM] * len(arrays),
            out_specs=[VMEM] * len(outs),
            scratch_shapes=scratch,
            compiler_params=PARAMS,
            cost_estimate=pl.CostEstimate(flops=cost, bytes_accessed=cost, transcendentals=0),
        )(*scalars, *arrays)

    def react_and_prepare(u, prepare, olds):
        kernel = functools.partial(reaction_kernel, prepare, len(olds))
        return call(kernel, [state, state], (), (u, mix, *olds))

    def move_and_prepare(step, arrays, prepare, olds, keep):
        inputs = len(arrays) + len(olds)
        kernel = functools.partial(moved_reaction_kernel, step, prepare, len(arrays), inputs, keep)
        outs = [state, state, rounded] + [state] * keep
        return call(kernel, outs, (flags,), (mix, *arrays, *olds))

    def moved_packs(step, arrays):
        kernel = functools.partial(moved_pack_kernel, step, len(arrays))
        return call(kernel, rims, (flags,), arrays)

    def force(received, vb, part, weight=None, base=None, keep=True, shift=False, send=False):
        outs = [state] * keep + [shifted] * shift + [state] * (weight is not None)
        if send:
            outs += [rounded] + rims
        kernel = functools.partial(force_kernel, weight, keep, shift, send)
        base = () if weight is None else (base,)
        return call(kernel, outs, (flags, table), (vb, part, *received, coeffs, *base), ext)

    h, gaps = step_size, node_gaps
    vb, *packs = call(first_kernel, [rounded] + rims, (flags,), (first,))
    received = exchange(packs)
    split = jax.ShapeDtypeStruct((species, 3 * species), bf16)
    part, mix = call(first_reaction_kernel, [state, split], (), (first, mixing, coeffs))
    f, fb = force(received, vb, part, shift=True)

    arrays = (first, next_slice(first), f, next_slice(fb))
    received = exchange(moved_packs(early_step, arrays))
    part, base, vb, e0 = move_and_prepare(early_step, arrays, prepare_first(1), (f,), True)
    e1, u, vb, *packs = force(received, vb, part, h * gaps[1], base, send=True)

    received = exchange(packs)
    part, base = react_and_prepare(u, prepare_first(2), (f,))
    e2, u, vb, *packs = force(received, vb, part, h * gaps[2], base, send=True)

    came = next_slice(u)
    received = exchange(packs)
    part, base = react_and_prepare(u, prepare_late, (e0, e1, e2))
    e3, e3b, olds = force(received, vb, part, h * node_integrals[0][2], base, shift=True)

    arrays = (first, came, e0, next_slice(e3b), olds)
    received = exchange(moved_packs(late_step, arrays))
    olds = (e1, e2, e3)
    part, base, vb = move_and_prepare(late_step, arrays, prepare_second(1), olds, False)
    u, vb, *packs = force(received, vb, part, h * gaps[1], base, keep=False, send=True)

    received = exchange(packs)
    part, base = react_and_prepare(u, prepare_second(2), olds)
    (end,) = force(received, vb, part, h * gaps[2], base, keep=False)
    return jnp.transpose(end, (1, 0, 2))[None]


def solution(mesh):
    placed = (
        P("tm", None, "space", None),
        P(),
        P("space", None),
        P("space", None),
        P("space", None),
        P(),
    )
    return jax.shard_map(
        per_device,
        mesh=mesh,
        in_specs=placed,
        out_specs=P("tm", None, "space", None),
        check_vma=False,
    )
```

```python
import functools
import math

import jax
import jax.numpy as jnp
from jax import lax
from jax.experimental import pallas as pl
from jax.experimental.pallas import tpu as pltpu
from jax.sharding import PartitionSpec as P

SWEEPS = 2

step_size = 0.3
root_six = math.sqrt(6.0)
node_times = ((4.0 - root_six) / 10.0, (4.0 + root_six) / 10.0, 1.0)
radau_rows = (
    (
        (88.0 - 7.0 * root_six) / 360.0,
        (296.0 - 169.0 * root_six) / 1800.0,
        (-2.0 + 3.0 * root_six) / 225.0,
    ),
    (
        (296.0 + 169.0 * root_six) / 1800.0,
        (88.0 + 7.0 * root_six) / 360.0,
        (-2.0 - 3.0 * root_six) / 225.0,
    ),
    ((16.0 - root_six) / 36.0, (16.0 + root_six) / 36.0, 1.0 / 9.0),
)
node_gaps = (node_times[0], node_times[1] - node_times[0], node_times[2] - node_times[1])
node_integrals = (
    radau_rows[0],
    tuple((radau_rows[1][j] - radau_rows[0][j] for j in range(3))),
    tuple((radau_rows[2][j] - radau_rows[1][j] for j in range(3))),
)

f32 = jnp.float32
bf16 = jnp.bfloat16
VMEM = pl.BlockSpec(memory_space=pltpu.VMEM)
SMEM = pl.BlockSpec(memory_space=pltpu.SMEM)
PARAMS = pltpu.CompilerParams(vmem_limit_bytes=8 * 1024 * 1024)
UNROLL = 32
TERMS = 8
WIDTH = 2 * TERMS


def pairing(slices, parts, distance, late):
    route = []
    for a in range(slices):
        for p in range(parts):
            ahead = ((p // distance) % 2 == 0) != late
            q = p + distance if ahead else p - distance
            b, q = (a, q) if 0 <= q < parts else (a ^ 1, p)
            route.append((a * parts + p, b * parts + q))
    return route


def swap(block, distance, late):
    route = pairing(lax.axis_size("tm"), lax.axis_size("space"), distance, late)
    return lax.ppermute(block, ("tm", "space"), route)


def next_slice(block):
    n = lax.axis_size("tm")
    return lax.ppermute(block, "tm", [(i, (i + 1) % n) for i in range(n)])


PLAN = 13
PAIRS = ((2, True), (2, False), (1, True), (1, False))


def exchange(packs):
    return tuple(swap(x, d, late) for x, (d, late) in zip(packs, PAIRS))


def plan():
    p = lax.axis_index("space")
    n = lax.axis_size("space")
    sends, fills, valid = [], [], []
    for distance, late in PAIRS:
        base = 0 if distance == 1 else 2
        ahead = ((p // distance) % 2 == 0) != late
        q = jnp.where(ahead, p + distance, p - distance)
        sends.append(jnp.where(ahead, base, base + 1))
        fills.append(jnp.where(ahead, base + 1, base))
        valid.append((q >= 0) & (q < n))
    leading = lax.axis_index("tm") == 0
    return jnp.stack([x.astype(jnp.int32) for x in sends + fills + valid + [leading]])


def pack(flags, vb, packs):
    slots = packs[0].shape[0]
    for k, out in enumerate(packs):
        first = PLAN + flags[k] * slots
        for j in range(slots):
            out[j] = vb[flags[first + j]]


def first_kernel(flags, u, vb, *packs):
    nblocks = u.shape[0]
    vb[0:nblocks] = u[...].astype(bf16)
    vb[nblocks] = jnp.zeros(vb.shape[1:], bf16)
    pack(flags, vb, packs)


def react(mix, field):
    th = jnp.tanh(field)
    hi = th.astype(bf16)
    lo = (th - hi.astype(f32)).astype(bf16)
    return jnp.dot(mix, jnp.concatenate([hi, hi, lo], axis=0), preferred_element_type=f32)


def per_block(count, body):
    def several(i, carry):
        for j in range(UNROLL):
            body(i * UNROLL + j)
        return carry

    lax.fori_loop(0, count // UNROLL, several, 0)


def local_terms(table, coeffs, vb, b):
    nblocks = vb.shape[0] - 1
    at = b * WIDTH
    other = jnp.minimum(table[at + TERMS], nblocks)
    return jnp.dot(
        jnp.concatenate([vb[b], vb[other]], axis=1),
        jnp.concatenate([coeffs[table[at]], coeffs[table[at + 1]]], axis=0),
        preferred_element_type=f32,
    )


def first_reaction_kernel(u, mixing, coeffs, part, mix):
    del coeffs
    m = mixing[...]
    m_hi = m.astype(bf16)
    m_lo = (m - m_hi.astype(f32)).astype(bf16)
    mix[...] = jnp.concatenate([m_hi, m_lo, m_hi], axis=1)
    mixv = mix[...]

    def body(b):
        part[b] = react(mixv, u[b])

    per_block(u.shape[0], body)


def table_kernel(given, after, table, mark):
    nblocks = after.shape[0]
    mark[...] = jnp.zeros_like(mark)

    def body(b, count):
        source, at = b * (WIDTH - 1), b * WIDTH
        values = [given[source + t] for t in range(WIDTH - 1)]
        mats, cols = values[1:TERMS], values[TERMS:]
        chosen, mat, col = jnp.int32(0), mats[0], cols[0]
        lonely = jnp.int32(1)
        for t in reversed(range(TERMS - 1)):
            local = cols[t] < nblocks
            chosen = jnp.where(local, t, chosen)
            mat = jnp.where(local, mats[t], mat)
            col = jnp.where(local, cols[t], col)
            lonely = jnp.where(local, 0, lonely)
        table[at] = values[0]
        table[at + 1] = mat
        table[at + TERMS] = col
        for t in range(1, TERMS - 1):
            here = chosen == t
            table[at + 1 + t] = jnp.where(here, mats[0], mats[t])
            table[at + TERMS + t] = jnp.where(here, cols[0], cols[t])
        table[count * WIDTH + WIDTH - 1] = b
        return count + lonely

    table[nblocks * WIDTH] = lax.fori_loop(0, nblocks, body, jnp.int32(0), unroll=4)


def reaction_kernel(prepare, extras, table, u, vb, mix, coeffs, *refs):
    olds, (part, base) = refs[:extras], refs[extras:]
    mixv = mix[...]

    def body(b):
        field = u[b]
        part[b] = react(mixv, field) + local_terms(table, coeffs, vb, b)
        base[b] = prepare(field, [old[b] for old in olds])

    per_block(u.shape[0], body)


def moved_pack_kernel(step, extras, flags, mark, *refs):
    del mark
    arrays, packs = refs[:extras], refs[extras:]
    nblocks = arrays[0].shape[0]
    slots = packs[0].shape[0]
    leading = flags[PLAN - 1] > 0

    def fill(lead):
        for k, out in enumerate(packs):
            first = PLAN + flags[k] * slots
            for j in range(slots):
                row = flags[first + j]
                block = step(lead, arrays, jnp.minimum(row, nblocks - 1))[0].astype(bf16)
                out[j] = jnp.where(row < nblocks, block, jnp.zeros_like(block))

    pl.when(leading)(lambda: fill(True))
    pl.when(jnp.logical_not(leading))(lambda: fill(False))


def moved_reaction_kernel(step, prepare, extras, inputs, keep, flags, table, mix, coeffs, *refs):
    arrays, olds, outs = refs[:extras], refs[extras:inputs], refs[inputs:]
    part, base, vb = outs[:3]
    nblocks = part.shape[0]
    leading = flags[PLAN - 1] > 0
    mixv = mix[...]
    vb[nblocks] = jnp.zeros(vb.shape[1:], bf16)

    def body(b):
        field, force = step(leading, arrays, b)
        if keep:
            outs[3][b] = force
        vb[b] = field.astype(bf16)
        part[b] = react(mixv, field)
        base[b] = prepare(field, [old[b] for old in olds])

    def add(b):
        part[b] += local_terms(table, coeffs, vb, b)

    per_block(nblocks, body)
    per_block(nblocks, add)


def force_kernel(weight, keep, shift, send, whole, flags, table, vb, part, *refs):
    received, refs = refs[:4], refs[4:]
    coeffs, refs = refs[0], refs[1:]
    if weight is not None:
        base, refs = refs[0], refs[1:]
    outs, ext = list(refs[:-1]), refs[-1]
    forces = outs.pop(0) if keep else None
    shifted = outs.pop(0) if shift else None
    states = outs.pop(0) if weight is not None else None
    rounded = outs.pop(0) if send else None
    nblocks = part.shape[0]
    slots = received[0].shape[0]
    ext[0:nblocks] = vb[0:nblocks]
    for k, got in enumerate(received):
        live = flags[8 + k] > 0
        block = got[...]
        ext[pl.ds(nblocks + flags[4 + k] * slots, slots)] = jnp.where(live, block, jnp.zeros_like(block))

    def body(b):
        if whole:
            at = b * (WIDTH - 1)
            xs = [vb[b]] + [ext[table[at + TERMS + t]] for t in range(TERMS - 1)]
            ws = [coeffs[table[at + t]] for t in range(TERMS)]
        else:
            at = b * WIDTH
            xs = [ext[table[at + TERMS + t]] for t in range(1, TERMS - 1)]
            ws = [coeffs[table[at + 1 + t]] for t in range(1, TERMS - 1)]
        force = part[b] + jnp.dot(
            jnp.concatenate(xs, axis=1), jnp.concatenate(ws, axis=0), preferred_element_type=f32
        )
        if keep:
            forces[b] = force
        if shift:
            shifted[b] = force.astype(bf16)
        if weight is not None:
            new = base[b] + weight * force
            states[b] = new
            if send:
                rounded[b] = new.astype(bf16)

    def late(i, carry):
        b = table[i * WIDTH + WIDTH - 1]
        at = b * WIDTH
        more = jnp.dot(ext[table[at + TERMS]], coeffs[table[at + 1]], preferred_element_type=f32)
        if keep:
            force = forces[b] + more
            forces[b] = force
            if shift:
                shifted[b] = force.astype(bf16)
        if weight is not None:
            new = states[b] + weight * more
            states[b] = new
            if send:
                rounded[b] = new.astype(bf16)
        return carry

    per_block(nblocks, body)
    if not whole:
        lax.fori_loop(0, table[nblocks * WIDTH], late, 0)
    if send:
        rounded[nblocks] = jnp.zeros(rounded.shape[1:], bf16)
        pack(flags, rounded, outs)


def pick(which, one, other):
    if isinstance(which, bool):
        return one() if which else other()
    return jnp.where(which, one(), other())


def early_step(leading, arrays, b):
    guess, incoming, force, moved = arrays
    g, q = node_gaps[0], sum(node_integrals[0])
    f = force[b]
    start = pick(leading, lambda: guess[b], lambda: incoming[b])
    e = pick(leading, lambda: f, lambda: moved[b].astype(f32))
    return start + step_size * (g * (e - f) + q * f), e


def late_step(leading, arrays, b):
    guess, incoming, force, moved, olds = arrays
    start = pick(leading, lambda: guess[b], lambda: incoming[b])
    e = pick(leading, lambda: force[b], lambda: moved[b].astype(f32))
    return start + olds[b] + (step_size * node_gaps[0]) * e, e


def prepare_first(node):
    g, q = node_gaps[node], sum(node_integrals[node])

    def prepare(u, olds):
        (f,) = olds
        return u + step_size * (q * f - g * f)

    return prepare


def prepare_second(node):
    g, q = node_gaps[node], node_integrals[node]

    def prepare(u, olds):
        quad = q[0] * olds[0] + q[1] * olds[1] + q[2] * olds[2]
        return u + step_size * (quad - g * olds[node - 1])

    return prepare


def prepare_late(u, olds):
    e0, e1, e2 = olds
    q = node_integrals[0]
    return step_size * (q[0] * e1 + q[1] * e2 - node_gaps[0] * e0)


def per_device(guess, coeffs, coef_index, neighbours, send_lists, mixing):
    first = jnp.transpose(guess[0], (1, 0, 2))
    nblocks, species, cells = first.shape
    slots = send_lists.shape[1]
    rows = jnp.where(send_lists < 0, nblocks, send_lists)
    flags = jnp.concatenate([plan(), rows.reshape(-1)])
    given = jnp.concatenate([coef_index, neighbours], axis=1).reshape(-1)

    state = jax.ShapeDtypeStruct((nblocks, species, cells), f32)
    shifted = jax.ShapeDtypeStruct((nblocks, species, cells), bf16)
    rounded = jax.ShapeDtypeStruct((nblocks + 1, species, cells), bf16)
    rims = [jax.ShapeDtypeStruct((slots, species, cells), bf16)] * 4
    ext = [pltpu.VMEM((nblocks + 4 * slots, species, cells), bf16)]

    def call(kernel, outs, scalars, arrays, scratch=(), cost=4_000_000):
        return pl.pallas_call(
            kernel,
            out_shape=outs,
            in_specs=[SMEM] * len(scalars) + [VMEM] * len(arrays),
            out_specs=[VMEM] * len(outs),
            scratch_shapes=scratch,
            compiler_params=PARAMS,
            cost_estimate=pl.CostEstimate(flops=cost, bytes_accessed=cost, transcendentals=0),
        )(*scalars, *arrays)

    def react_and_prepare(u, vb, prepare, olds):
        kernel = functools.partial(reaction_kernel, prepare, len(olds))
        return call(kernel, [state, state], (table,), (u, vb, mix, coeffs, *olds))

    def move_and_prepare(step, arrays, prepare, olds, keep):
        inputs = len(arrays) + len(olds)
        kernel = functools.partial(moved_reaction_kernel, step, prepare, len(arrays), inputs, keep)
        outs = [state, state, rounded] + [state] * keep
        return call(kernel, outs, (flags, table), (mix, coeffs, *arrays, *olds))

    def moved_packs(step, arrays):
        kernel = functools.partial(moved_pack_kernel, step, len(arrays))
        return call(kernel, rims, (flags,), (mark, *arrays))

    def force(received, vb, part, weight=None, base=None, keep=True, shift=False, send=False, whole=False):
        outs = [state] * keep + [shifted] * shift + [state] * (weight is not None)
        if send:
            outs += [rounded] + rims
        kernel = functools.partial(force_kernel, weight, keep, shift, send, whole)
        base = () if weight is None else (base,)
        terms = given if whole else table
        return call(kernel, outs, (flags, terms), (vb, part, *received, coeffs, *base), ext)

    h, gaps = step_size, node_gaps
    vb, *packs = call(first_kernel, [rounded] + rims, (flags,), (first,))
    received = exchange(packs)
    split = jax.ShapeDtypeStruct((species, 3 * species), bf16)
    part, mix = call(first_reaction_kernel, [state, split], (), (first, mixing, coeffs))
    f, fb = force(received, vb, part, shift=True, whole=True)
    table, mark = pl.pallas_call(
        table_kernel,
        out_shape=[jax.ShapeDtypeStruct((nblocks * WIDTH + 1,), jnp.int32), jax.ShapeDtypeStruct((8, 128), f32)],
        in_specs=[SMEM, VMEM],
        out_specs=[SMEM, VMEM],
        compiler_params=PARAMS,
        cost_estimate=pl.CostEstimate(flops=1_000_000, bytes_accessed=1_000_000, transcendentals=0),
    )(given, f)

    arrays = (first, next_slice(first), f, next_slice(fb))
    received = exchange(moved_packs(early_step, arrays))
    part, base, vb, e0 = move_and_prepare(early_step, arrays, prepare_first(1), (f,), True)
    e1, u, vb, *packs = force(received, vb, part, h * gaps[1], base, send=True)

    received = exchange(packs)
    part, base = react_and_prepare(u, vb, prepare_first(2), (f,))
    e2, u, vb, *packs = force(received, vb, part, h * gaps[2], base, send=True)

    came = next_slice(u)
    received = exchange(packs)
    part, base = react_and_prepare(u, vb, prepare_late, (e0, e1, e2))
    e3, e3b, olds = force(received, vb, part, h * node_integrals[0][2], base, shift=True)

    arrays = (first, came, e0, next_slice(e3b), olds)
    received = exchange(moved_packs(late_step, arrays))
    olds = (e1, e2, e3)
    part, base, vb = move_and_prepare(late_step, arrays, prepare_second(1), olds, False)
    u, vb, *packs = force(received, vb, part, h * gaps[1], base, keep=False, send=True)

    received = exchange(packs)
    part, base = react_and_prepare(u, vb, prepare_second(2), olds)
    (end,) = force(received, vb, part, h * gaps[2], base, keep=False)
    return jnp.transpose(end, (1, 0, 2))[None]


def solution(mesh):
    placed = (
        P("tm", None, "space", None),
        P(),
        P("space", None),
        P("space", None),
        P("space", None),
        P(),
    )
    return jax.shard_map(
        per_device,
        mesh=mesh,
        in_specs=placed,
        out_specs=P("tm", None, "space", None),
        check_vma=False,
    )
```

```python
import functools
import math

import jax
import jax.numpy as jnp
from jax import lax
from jax.experimental import pallas as pl
from jax.experimental.pallas import tpu as pltpu
from jax.sharding import PartitionSpec as P

SWEEPS = 2

step_size = 0.3
root_six = math.sqrt(6.0)
node_times = ((4.0 - root_six) / 10.0, (4.0 + root_six) / 10.0, 1.0)
radau_rows = (
    (
        (88.0 - 7.0 * root_six) / 360.0,
        (296.0 - 169.0 * root_six) / 1800.0,
        (-2.0 + 3.0 * root_six) / 225.0,
    ),
    (
        (296.0 + 169.0 * root_six) / 1800.0,
        (88.0 + 7.0 * root_six) / 360.0,
        (-2.0 - 3.0 * root_six) / 225.0,
    ),
    ((16.0 - root_six) / 36.0, (16.0 + root_six) / 36.0, 1.0 / 9.0),
)
node_gaps = (node_times[0], node_times[1] - node_times[0], node_times[2] - node_times[1])
node_integrals = (
    radau_rows[0],
    tuple((radau_rows[1][j] - radau_rows[0][j] for j in range(3))),
    tuple((radau_rows[2][j] - radau_rows[1][j] for j in range(3))),
)

f32 = jnp.float32
bf16 = jnp.bfloat16
VMEM = pl.BlockSpec(memory_space=pltpu.VMEM)
SMEM = pl.BlockSpec(memory_space=pltpu.SMEM)
PARAMS = pltpu.CompilerParams(vmem_limit_bytes=8 * 1024 * 1024)
UNROLL = 32
TERMS = 8
WIDTH = 2 * TERMS


def pairing(slices, parts, distance, late):
    route = []
    for a in range(slices):
        for p in range(parts):
            ahead = ((p // distance) % 2 == 0) != late
            q = p + distance if ahead else p - distance
            b, q = (a, q) if 0 <= q < parts else (a ^ 1, p)
            route.append((a * parts + p, b * parts + q))
    return route


def swap(block, distance, late):
    route = pairing(lax.axis_size("tm"), lax.axis_size("space"), distance, late)
    return lax.ppermute(block, ("tm", "space"), route)


def next_slice(block):
    n = lax.axis_size("tm")
    return lax.ppermute(block, "tm", [(i, (i + 1) % n) for i in range(n)])


PLAN = 13
PAIRS = ((2, True), (2, False), (1, True), (1, False))


def exchange(packs):
    return tuple(swap(x, d, late) for x, (d, late) in zip(packs, PAIRS))


def plan():
    p = lax.axis_index("space")
    n = lax.axis_size("space")
    sends, fills, valid = [], [], []
    for distance, late in PAIRS:
        base = 0 if distance == 1 else 2
        ahead = ((p // distance) % 2 == 0) != late
        q = jnp.where(ahead, p + distance, p - distance)
        sends.append(jnp.where(ahead, base, base + 1))
        fills.append(jnp.where(ahead, base + 1, base))
        valid.append((q >= 0) & (q < n))
    leading = lax.axis_index("tm") == 0
    return jnp.stack([x.astype(jnp.int32) for x in sends + fills + valid + [leading]])


def pack(flags, vb, packs):
    slots = packs[0].shape[0]
    for k, out in enumerate(packs):
        first = PLAN + flags[k] * slots
        for j in range(slots):
            out[j] = vb[flags[first + j]]


def first_kernel(flags, u, vb, *packs):
    nblocks = u.shape[0]
    vb[0:nblocks] = u[...].astype(bf16)
    vb[nblocks] = jnp.zeros(vb.shape[1:], bf16)
    pack(flags, vb, packs)


def react(mix, field):
    th = jnp.tanh(field)
    hi = th.astype(bf16)
    lo = (th - hi.astype(f32)).astype(bf16)
    return jnp.dot(mix, jnp.concatenate([hi, hi, lo], axis=0), preferred_element_type=f32)


def per_block(count, body):
    def several(i, carry):
        for j in range(UNROLL):
            body(i * UNROLL + j)
        return carry

    lax.fori_loop(0, count // UNROLL, several, 0)


def local_terms(table, coeffs, vb, b):
    nblocks = vb.shape[0] - 1
    at = b * WIDTH
    other = jnp.minimum(table[at + TERMS], nblocks)
    return jnp.dot(
        jnp.concatenate([vb[b], vb[other]], axis=1),
        jnp.concatenate([coeffs[table[at]], coeffs[table[at + 1]]], axis=0),
        preferred_element_type=f32,
    )


def first_reaction_kernel(u, mixing, coeffs, part, mix, matrices, arrival):
    fetch = pltpu.make_async_copy(coeffs, matrices, arrival)
    fetch.start()
    m = mixing[...]
    m_hi = m.astype(bf16)
    m_lo = (m - m_hi.astype(f32)).astype(bf16)
    mix[...] = jnp.concatenate([m_hi, m_lo, m_hi], axis=1)
    mixv = mix[...]

    def body(b):
        part[b] = react(mixv, u[b])

    per_block(u.shape[0], body)
    fetch.wait()


def table_kernel(given, after, table, mark):
    nblocks = after.shape[0]
    mark[...] = jnp.zeros_like(mark)

    def body(b, count):
        source, at = b * (WIDTH - 1), b * WIDTH
        values = [given[source + t] for t in range(WIDTH - 1)]
        mats, cols = values[1:TERMS], values[TERMS:]
        chosen, mat, col = jnp.int32(0), mats[0], cols[0]
        lonely = jnp.int32(1)
        for t in reversed(range(TERMS - 1)):
            local = cols[t] < nblocks
            chosen = jnp.where(local, t, chosen)
            mat = jnp.where(local, mats[t], mat)
            col = jnp.where(local, cols[t], col)
            lonely = jnp.where(local, 0, lonely)
        table[at] = values[0]
        table[at + 1] = mat
        table[at + TERMS] = col
        for t in range(1, TERMS - 1):
            here = chosen == t
            table[at + 1 + t] = jnp.where(here, mats[0], mats[t])
            table[at + TERMS + t] = jnp.where(here, cols[0], cols[t])
        table[count * WIDTH + WIDTH - 1] = b
        return count + lonely

    table[nblocks * WIDTH] = lax.fori_loop(0, nblocks, body, jnp.int32(0), unroll=4)


def reaction_kernel(prepare, extras, table, u, vb, mix, coeffs, *refs):
    olds, (part, base) = refs[:extras], refs[extras:]
    mixv = mix[...]

    def body(b):
        field = u[b]
        part[b] = react(mixv, field) + local_terms(table, coeffs, vb, b)
        base[b] = prepare(field, [old[b] for old in olds])

    per_block(u.shape[0], body)


def moved_pack_kernel(step, extras, flags, mark, *refs):
    del mark
    arrays, packs = refs[:extras], refs[extras:]
    nblocks = arrays[0].shape[0]
    slots = packs[0].shape[0]
    leading = flags[PLAN - 1] > 0

    def fill(lead):
        for k, out in enumerate(packs):
            first = PLAN + flags[k] * slots
            for j in range(slots):
                row = flags[first + j]
                block = step(lead, arrays, jnp.minimum(row, nblocks - 1))[0].astype(bf16)
                out[j] = jnp.where(row < nblocks, block, jnp.zeros_like(block))

    pl.when(leading)(lambda: fill(True))
    pl.when(jnp.logical_not(leading))(lambda: fill(False))


def moved_reaction_kernel(step, prepare, extras, inputs, keep, flags, table, mix, coeffs, *refs):
    arrays, olds, outs = refs[:extras], refs[extras:inputs], refs[inputs:]
    part, base, vb = outs[:3]
    nblocks = part.shape[0]
    leading = flags[PLAN - 1] > 0
    mixv = mix[...]
    vb[nblocks] = jnp.zeros(vb.shape[1:], bf16)

    def body(b):
        field, force = step(leading, arrays, b)
        if keep:
            outs[3][b] = force
        vb[b] = field.astype(bf16)
        part[b] = react(mixv, field)
        base[b] = prepare(field, [old[b] for old in olds])

    def add(b):
        part[b] += local_terms(table, coeffs, vb, b)

    per_block(nblocks, body)
    per_block(nblocks, add)


def force_kernel(weight, keep, shift, send, whole, flags, table, vb, part, *refs):
    received, refs = refs[:4], refs[4:]
    coeffs, refs = refs[0], refs[1:]
    if weight is not None:
        base, refs = refs[0], refs[1:]
    outs, ext = list(refs[:-1]), refs[-1]
    forces = outs.pop(0) if keep else None
    shifted = outs.pop(0) if shift else None
    states = outs.pop(0) if weight is not None else None
    rounded = outs.pop(0) if send else None
    nblocks = part.shape[0]
    slots = received[0].shape[0]
    ext[0:nblocks] = vb[0:nblocks]
    for k, got in enumerate(received):
        live = flags[8 + k] > 0
        block = got[...]
        ext[pl.ds(nblocks + flags[4 + k] * slots, slots)] = jnp.where(live, block, jnp.zeros_like(block))

    def body(b):
        if whole:
            at = b * (WIDTH - 1)
            xs = [vb[b]] + [ext[table[at + TERMS + t]] for t in range(TERMS - 1)]
            ws = [coeffs[table[at + t]] for t in range(TERMS)]
        else:
            at = b * WIDTH
            xs = [ext[table[at + TERMS + t]] for t in range(1, TERMS - 1)]
            ws = [coeffs[table[at + 1 + t]] for t in range(1, TERMS - 1)]
        force = part[b] + jnp.dot(
            jnp.concatenate(xs, axis=1), jnp.concatenate(ws, axis=0), preferred_element_type=f32
        )
        if keep:
            forces[b] = force
        if shift:
            shifted[b] = force.astype(bf16)
        if weight is not None:
            new = base[b] + weight * force
            states[b] = new
            if send:
                rounded[b] = new.astype(bf16)

    def late(i, carry):
        b = table[i * WIDTH + WIDTH - 1]
        at = b * WIDTH
        more = jnp.dot(ext[table[at + TERMS]], coeffs[table[at + 1]], preferred_element_type=f32)
        if keep:
            force = forces[b] + more
            forces[b] = force
            if shift:
                shifted[b] = force.astype(bf16)
        if weight is not None:
            new = states[b] + weight * more
            states[b] = new
            if send:
                rounded[b] = new.astype(bf16)
        return carry

    per_block(nblocks, body)
    if not whole:
        lax.fori_loop(0, table[nblocks * WIDTH], late, 0)
    if send:
        rounded[nblocks] = jnp.zeros(rounded.shape[1:], bf16)
        pack(flags, rounded, outs)


def pick(which, one, other):
    if isinstance(which, bool):
        return one() if which else other()
    return jnp.where(which, one(), other())


def early_step(leading, arrays, b):
    guess, incoming, force, moved = arrays
    g, q = node_gaps[0], sum(node_integrals[0])
    f = force[b]
    start = pick(leading, lambda: guess[b], lambda: incoming[b])
    e = pick(leading, lambda: f, lambda: moved[b].astype(f32))
    return start + step_size * (g * (e - f) + q * f), e


def late_step(leading, arrays, b):
    guess, incoming, force, moved, olds = arrays
    start = pick(leading, lambda: guess[b], lambda: incoming[b])
    e = pick(leading, lambda: force[b], lambda: moved[b].astype(f32))
    return start + olds[b] + (step_size * node_gaps[0]) * e, e


def prepare_first(node):
    g, q = node_gaps[node], sum(node_integrals[node])

    def prepare(u, olds):
        (f,) = olds
        return u + step_size * (q * f - g * f)

    return prepare


def prepare_second(node):
    g, q = node_gaps[node], node_integrals[node]

    def prepare(u, olds):
        quad = q[0] * olds[0] + q[1] * olds[1] + q[2] * olds[2]
        return u + step_size * (quad - g * olds[node - 1])

    return prepare


def prepare_late(u, olds):
    e0, e1, e2 = olds
    q = node_integrals[0]
    return step_size * (q[0] * e1 + q[1] * e2 - node_gaps[0] * e0)


def per_device(guess, coeffs, coef_index, neighbours, send_lists, mixing):
    first = jnp.transpose(guess[0], (1, 0, 2))
    nblocks, species, cells = first.shape
    slots = send_lists.shape[1]
    rows = jnp.where(send_lists < 0, nblocks, send_lists)
    flags = jnp.concatenate([plan(), rows.reshape(-1)])
    given = jnp.concatenate([coef_index, neighbours], axis=1).reshape(-1)

    state = jax.ShapeDtypeStruct((nblocks, species, cells), f32)
    shifted = jax.ShapeDtypeStruct((nblocks, species, cells), bf16)
    rounded = jax.ShapeDtypeStruct((nblocks + 1, species, cells), bf16)
    rims = [jax.ShapeDtypeStruct((slots, species, cells), bf16)] * 4
    ext = [pltpu.VMEM((nblocks + 4 * slots, species, cells), bf16)]

    def call(kernel, outs, scalars, arrays, scratch=(), cost=4_000_000):
        return pl.pallas_call(
            kernel,
            out_shape=outs,
            in_specs=[SMEM] * len(scalars) + [VMEM] * len(arrays),
            out_specs=[VMEM] * len(outs),
            scratch_shapes=scratch,
            compiler_params=PARAMS,
            cost_estimate=pl.CostEstimate(flops=cost, bytes_accessed=cost, transcendentals=0),
        )(*scalars, *arrays)

    def react_and_prepare(u, vb, prepare, olds):
        kernel = functools.partial(reaction_kernel, prepare, len(olds))
        return call(kernel, [state, state], (table,), (u, vb, mix, coeffs, *olds))

    def move_and_prepare(step, arrays, prepare, olds, keep):
        inputs = len(arrays) + len(olds)
        kernel = functools.partial(moved_reaction_kernel, step, prepare, len(arrays), inputs, keep)
        outs = [state, state, rounded] + [state] * keep
        return call(kernel, outs, (flags, table), (mix, coeffs, *arrays, *olds))

    def moved_packs(step, arrays):
        kernel = functools.partial(moved_pack_kernel, step, len(arrays))
        return call(kernel, rims, (flags,), (mark, *arrays))

    def force(received, vb, part, weight=None, base=None, keep=True, shift=False, send=False, whole=False):
        outs = [state] * keep + [shifted] * shift + [state] * (weight is not None)
        if send:
            outs += [rounded] + rims
        kernel = functools.partial(force_kernel, weight, keep, shift, send, whole)
        base = () if weight is None else (base,)
        terms = given if whole else table
        return call(kernel, outs, (flags, terms), (vb, part, *received, coeffs, *base), ext)

    h, gaps = step_size, node_gaps
    vb, *packs = call(first_kernel, [rounded] + rims, (flags,), (first,))
    received = exchange(packs)
    split = jax.ShapeDtypeStruct((species, 3 * species), bf16)
    part, mix, coeffs = pl.pallas_call(
        first_reaction_kernel,
        out_shape=[state, split, jax.ShapeDtypeStruct(coeffs.shape, bf16)],
        in_specs=[VMEM, VMEM, pl.BlockSpec(memory_space=pltpu.HBM)],
        out_specs=[VMEM] * 3,
        scratch_shapes=[pltpu.SemaphoreType.DMA],
        compiler_params=pltpu.CompilerParams(vmem_limit_bytes=48 * 1024 * 1024),
        cost_estimate=pl.CostEstimate(flops=4_000_000, bytes_accessed=4_000_000, transcendentals=0),
    )(first, mixing, coeffs)
    f, fb = force(received, vb, part, shift=True, whole=True)
    table, mark = pl.pallas_call(
        table_kernel,
        out_shape=[jax.ShapeDtypeStruct((nblocks * WIDTH + 1,), jnp.int32), jax.ShapeDtypeStruct((8, 128), f32)],
        in_specs=[SMEM, VMEM],
        out_specs=[SMEM, VMEM],
        compiler_params=PARAMS,
        cost_estimate=pl.CostEstimate(flops=1_000_000, bytes_accessed=1_000_000, transcendentals=0),
    )(given, f)

    arrays = (first, next_slice(first), f, next_slice(fb))
    received = exchange(moved_packs(early_step, arrays))
    part, base, vb, e0 = move_and_prepare(early_step, arrays, prepare_first(1), (f,), True)
    e1, u, vb, *packs = force(received, vb, part, h * gaps[1], base, send=True)

    received = exchange(packs)
    part, base = react_and_prepare(u, vb, prepare_first(2), (f,))
    e2, u, vb, *packs = force(received, vb, part, h * gaps[2], base, send=True)

    came = next_slice(u)
    received = exchange(packs)
    part, base = react_and_prepare(u, vb, prepare_late, (e0, e1, e2))
    e3, e3b, olds = force(received, vb, part, h * node_integrals[0][2], base, shift=True)

    arrays = (first, came, e0, next_slice(e3b), olds)
    received = exchange(moved_packs(late_step, arrays))
    olds = (e1, e2, e3)
    part, base, vb = move_and_prepare(late_step, arrays, prepare_second(1), olds, False)
    u, vb, *packs = force(received, vb, part, h * gaps[1], base, keep=False, send=True)

    received = exchange(packs)
    part, base = react_and_prepare(u, vb, prepare_second(2), olds)
    (end,) = force(received, vb, part, h * gaps[2], base, keep=False)
    return jnp.transpose(end, (1, 0, 2))[None]


def solution(mesh):
    placed = (
        P("tm", None, "space", None),
        P(),
        P("space", None),
        P("space", None),
        P("space", None),
        P(),
    )
    return jax.shard_map(
        per_device,
        mesh=mesh,
        in_specs=placed,
        out_specs=P("tm", None, "space", None),
        check_vma=False,
    )
```

```python
import functools
import math

import jax
import jax.numpy as jnp
from jax import lax
from jax.experimental import pallas as pl
from jax.experimental.pallas import tpu as pltpu
from jax.sharding import PartitionSpec as P

SWEEPS = 2

step_size = 0.3
root_six = math.sqrt(6.0)
node_times = ((4.0 - root_six) / 10.0, (4.0 + root_six) / 10.0, 1.0)
radau_rows = (
    (
        (88.0 - 7.0 * root_six) / 360.0,
        (296.0 - 169.0 * root_six) / 1800.0,
        (-2.0 + 3.0 * root_six) / 225.0,
    ),
    (
        (296.0 + 169.0 * root_six) / 1800.0,
        (88.0 + 7.0 * root_six) / 360.0,
        (-2.0 - 3.0 * root_six) / 225.0,
    ),
    ((16.0 - root_six) / 36.0, (16.0 + root_six) / 36.0, 1.0 / 9.0),
)
node_gaps = (node_times[0], node_times[1] - node_times[0], node_times[2] - node_times[1])
node_integrals = (
    radau_rows[0],
    tuple((radau_rows[1][j] - radau_rows[0][j] for j in range(3))),
    tuple((radau_rows[2][j] - radau_rows[1][j] for j in range(3))),
)

f32 = jnp.float32
bf16 = jnp.bfloat16
VMEM = pl.BlockSpec(memory_space=pltpu.VMEM)
SMEM = pl.BlockSpec(memory_space=pltpu.SMEM)
PARAMS = pltpu.CompilerParams(vmem_limit_bytes=8 * 1024 * 1024)
UNROLL = 32
TERMS = 8
WIDTH = 2 * TERMS


def pairing(slices, parts, distance, late):
    route = []
    for a in range(slices):
        for p in range(parts):
            ahead = ((p // distance) % 2 == 0) != late
            q = p + distance if ahead else p - distance
            b, q = (a, q) if 0 <= q < parts else (a ^ 1, p)
            route.append((a * parts + p, b * parts + q))
    return route


def swap(block, distance, late):
    route = pairing(lax.axis_size("tm"), lax.axis_size("space"), distance, late)
    return lax.ppermute(block, ("tm", "space"), route)


def next_slice(block):
    n = lax.axis_size("tm")
    return lax.ppermute(block, "tm", [(i, (i + 1) % n) for i in range(n)])


PLAN = 13
PAIRS = ((2, True), (2, False), (1, True), (1, False))


def exchange(packs):
    return tuple(swap(x, d, late) for x, (d, late) in zip(packs, PAIRS))


def plan():
    p = lax.axis_index("space")
    n = lax.axis_size("space")
    sends, fills, valid = [], [], []
    for distance, late in PAIRS:
        base = 0 if distance == 1 else 2
        ahead = ((p // distance) % 2 == 0) != late
        q = jnp.where(ahead, p + distance, p - distance)
        sends.append(jnp.where(ahead, base, base + 1))
        fills.append(jnp.where(ahead, base + 1, base))
        valid.append((q >= 0) & (q < n))
    leading = lax.axis_index("tm") == 0
    return jnp.stack([x.astype(jnp.int32) for x in sends + fills + valid + [leading]])


def pack(flags, vb, packs):
    slots = packs[0].shape[0]
    for k, out in enumerate(packs):
        first = PLAN + flags[k] * slots
        for j in range(slots):
            out[j] = vb[flags[first + j]]


def first_kernel(flags, u, vb, *packs):
    nblocks = u.shape[0]
    vb[0:nblocks] = u[...].astype(bf16)
    vb[nblocks] = jnp.zeros(vb.shape[1:], bf16)
    pack(flags, vb, packs)


def react(mix, field):
    th = jnp.tanh(field)
    hi = th.astype(bf16)
    lo = (th - hi.astype(f32)).astype(bf16)
    return jnp.dot(mix, jnp.concatenate([hi, hi, lo], axis=0), preferred_element_type=f32)


def per_block(count, body):
    def several(i, carry):
        for j in range(UNROLL):
            body(i * UNROLL + j)
        return carry

    lax.fori_loop(0, count // UNROLL, several, 0)


def local_terms(table, coeffs, vb, b):
    nblocks = vb.shape[0] - 1
    at = b * WIDTH
    other = jnp.minimum(table[at + TERMS], nblocks)
    return jnp.dot(
        jnp.concatenate([vb[b], vb[other]], axis=1),
        jnp.concatenate([coeffs[table[at]], coeffs[table[at + 1]]], axis=0),
        preferred_element_type=f32,
    )


def first_reaction_kernel(u, mixing, coeffs, part, mix, matrices, arrival):
    fetch = pltpu.make_async_copy(coeffs, matrices, arrival)
    fetch.start()
    m = mixing[...]
    m_hi = m.astype(bf16)
    m_lo = (m - m_hi.astype(f32)).astype(bf16)
    mix[...] = jnp.concatenate([m_hi, m_lo, m_hi], axis=1)
    mixv = mix[...]

    def body(b):
        part[b] = react(mixv, u[b])

    per_block(u.shape[0], body)
    fetch.wait()


def table_kernel(given, after, table, mark):
    nblocks = after.shape[0]
    mark[...] = jnp.zeros_like(mark)

    def body(b, count):
        source, at = b * (WIDTH - 1), b * WIDTH
        values = [given[source + t] for t in range(WIDTH - 1)]
        mats, cols = values[1:TERMS], values[TERMS:]
        chosen, mat, col = jnp.int32(TERMS), mats[0], cols[0]
        for t in reversed(range(TERMS - 1)):
            local = cols[t] < nblocks
            chosen = jnp.where(local, t, chosen)
            mat = jnp.where(local, mats[t], mat)
            col = jnp.where(local, cols[t], col)
        lonely = chosen == TERMS
        chosen = jnp.where(lonely, 0, chosen)
        table[at] = values[0]
        for t in range(1, TERMS - 1):
            table[at + 1 + t] = mats[t]
            table[at + TERMS + t] = cols[t]
        table[at + 1 + chosen] = mats[0]
        table[at + TERMS + chosen] = cols[0]
        table[at + 1] = mat
        table[at + TERMS] = col
        table[count * WIDTH + WIDTH - 1] = b
        return count + lonely.astype(jnp.int32)

    table[nblocks * WIDTH] = lax.fori_loop(0, nblocks, body, jnp.int32(0), unroll=4)


def reaction_kernel(prepare, extras, table, u, vb, mix, coeffs, *refs):
    olds, (part, base) = refs[:extras], refs[extras:]
    mixv = mix[...]

    def body(b):
        field = u[b]
        part[b] = react(mixv, field) + local_terms(table, coeffs, vb, b)
        base[b] = prepare(field, [old[b] for old in olds])

    per_block(u.shape[0], body)


def moved_pack_kernel(step, extras, flags, mark, *refs):
    del mark
    arrays, packs = refs[:extras], refs[extras:]
    nblocks = arrays[0].shape[0]
    slots = packs[0].shape[0]
    leading = flags[PLAN - 1] > 0

    def fill(lead):
        for k, out in enumerate(packs):
            first = PLAN + flags[k] * slots
            for j in range(slots):
                row = flags[first + j]
                block = step(lead, arrays, jnp.minimum(row, nblocks - 1))[0].astype(bf16)
                out[j] = jnp.where(row < nblocks, block, jnp.zeros_like(block))

    pl.when(leading)(lambda: fill(True))
    pl.when(jnp.logical_not(leading))(lambda: fill(False))


def moved_reaction_kernel(step, prepare, extras, inputs, keep, flags, table, mix, coeffs, *refs):
    arrays, olds, outs = refs[:extras], refs[extras:inputs], refs[inputs:]
    part, base, vb = outs[:3]
    nblocks = part.shape[0]
    leading = flags[PLAN - 1] > 0
    mixv = mix[...]
    vb[nblocks] = jnp.zeros(vb.shape[1:], bf16)

    def body(b):
        field, force = step(leading, arrays, b)
        if keep:
            outs[3][b] = force
        vb[b] = field.astype(bf16)
        part[b] = react(mixv, field)
        base[b] = prepare(field, [old[b] for old in olds])

    def add(b):
        part[b] += local_terms(table, coeffs, vb, b)

    per_block(nblocks, body)
    per_block(nblocks, add)


def force_kernel(weight, keep, shift, send, whole, flags, table, vb, part, *refs):
    received, refs = refs[:4], refs[4:]
    coeffs, refs = refs[0], refs[1:]
    if weight is not None:
        base, refs = refs[0], refs[1:]
    outs, ext = list(refs[:-1]), refs[-1]
    forces = outs.pop(0) if keep else None
    shifted = outs.pop(0) if shift else None
    states = outs.pop(0) if weight is not None else None
    rounded = outs.pop(0) if send else None
    nblocks = part.shape[0]
    slots = received[0].shape[0]
    ext[0:nblocks] = vb[0:nblocks]
    for k, got in enumerate(received):
        live = flags[8 + k] > 0
        block = got[...]
        ext[pl.ds(nblocks + flags[4 + k] * slots, slots)] = jnp.where(live, block, jnp.zeros_like(block))

    def body(b):
        if whole:
            at = b * (WIDTH - 1)
            xs = [vb[b]] + [ext[table[at + TERMS + t]] for t in range(TERMS - 1)]
            ws = [coeffs[table[at + t]] for t in range(TERMS)]
        else:
            at = b * WIDTH
            xs = [ext[table[at + TERMS + t]] for t in range(1, TERMS - 1)]
            ws = [coeffs[table[at + 1 + t]] for t in range(1, TERMS - 1)]
        force = part[b] + jnp.dot(
            jnp.concatenate(xs, axis=1), jnp.concatenate(ws, axis=0), preferred_element_type=f32
        )
        if keep:
            forces[b] = force
        if shift:
            shifted[b] = force.astype(bf16)
        if weight is not None:
            new = base[b] + weight * force
            states[b] = new
            if send:
                rounded[b] = new.astype(bf16)

    def late(i, carry):
        b = table[i * WIDTH + WIDTH - 1]
        at = b * WIDTH
        more = jnp.dot(ext[table[at + TERMS]], coeffs[table[at + 1]], preferred_element_type=f32)
        if keep:
            force = forces[b] + more
            forces[b] = force
            if shift:
                shifted[b] = force.astype(bf16)
        if weight is not None:
            new = states[b] + weight * more
            states[b] = new
            if send:
                rounded[b] = new.astype(bf16)
        return carry

    per_block(nblocks, body)
    if not whole:
        lax.fori_loop(0, table[nblocks * WIDTH], late, 0)
    if send:
        rounded[nblocks] = jnp.zeros(rounded.shape[1:], bf16)
        pack(flags, rounded, outs)


def pick(which, one, other):
    if isinstance(which, bool):
        return one() if which else other()
    return jnp.where(which, one(), other())


def early_step(leading, arrays, b):
    guess, incoming, force, moved = arrays
    g, q = node_gaps[0], sum(node_integrals[0])
    f = force[b]
    start = pick(leading, lambda: guess[b], lambda: incoming[b])
    e = pick(leading, lambda: f, lambda: moved[b].astype(f32))
    return start + step_size * (g * (e - f) + q * f), e


def late_step(leading, arrays, b):
    guess, incoming, force, moved, olds = arrays
    start = pick(leading, lambda: guess[b], lambda: incoming[b])
    e = pick(leading, lambda: force[b], lambda: moved[b].astype(f32))
    return start + olds[b] + (step_size * node_gaps[0]) * e, e


def prepare_first(node):
    g, q = node_gaps[node], sum(node_integrals[node])

    def prepare(u, olds):
        (f,) = olds
        return u + step_size * (q * f - g * f)

    return prepare


def prepare_second(node):
    g, q = node_gaps[node], node_integrals[node]

    def prepare(u, olds):
        quad = q[0] * olds[0] + q[1] * olds[1] + q[2] * olds[2]
        return u + step_size * (quad - g * olds[node - 1])

    return prepare


def prepare_late(u, olds):
    e0, e1, e2 = olds
    q = node_integrals[0]
    return step_size * (q[0] * e1 + q[1] * e2 - node_gaps[0] * e0)


def per_device(guess, coeffs, coef_index, neighbours, send_lists, mixing):
    first = jnp.transpose(guess[0], (1, 0, 2))
    nblocks, species, cells = first.shape
    slots = send_lists.shape[1]
    rows = jnp.where(send_lists < 0, nblocks, send_lists)
    flags = jnp.concatenate([plan(), rows.reshape(-1)])
    given = jnp.concatenate([coef_index, neighbours], axis=1).reshape(-1)

    state = jax.ShapeDtypeStruct((nblocks, species, cells), f32)
    shifted = jax.ShapeDtypeStruct((nblocks, species, cells), bf16)
    rounded = jax.ShapeDtypeStruct((nblocks + 1, species, cells), bf16)
    rims = [jax.ShapeDtypeStruct((slots, species, cells), bf16)] * 4
    ext = [pltpu.VMEM((nblocks + 4 * slots, species, cells), bf16)]

    def call(kernel, outs, scalars, arrays, scratch=(), cost=4_000_000):
        return pl.pallas_call(
            kernel,
            out_shape=outs,
            in_specs=[SMEM] * len(scalars) + [VMEM] * len(arrays),
            out_specs=[VMEM] * len(outs),
            scratch_shapes=scratch,
            compiler_params=PARAMS,
            cost_estimate=pl.CostEstimate(flops=cost, bytes_accessed=cost, transcendentals=0),
        )(*scalars, *arrays)

    def react_and_prepare(u, vb, prepare, olds):
        kernel = functools.partial(reaction_kernel, prepare, len(olds))
        return call(kernel, [state, state], (table,), (u, vb, mix, coeffs, *olds))

    def move_and_prepare(step, arrays, prepare, olds, keep):
        inputs = len(arrays) + len(olds)
        kernel = functools.partial(moved_reaction_kernel, step, prepare, len(arrays), inputs, keep)
        outs = [state, state, rounded] + [state] * keep
        return call(kernel, outs, (flags, table), (mix, coeffs, *arrays, *olds))

    def moved_packs(step, arrays):
        kernel = functools.partial(moved_pack_kernel, step, len(arrays))
        return call(kernel, rims, (flags,), (mark, *arrays))

    def force(received, vb, part, weight=None, base=None, keep=True, shift=False, send=False, whole=False):
        outs = [state] * keep + [shifted] * shift + [state] * (weight is not None)
        if send:
            outs += [rounded] + rims
        kernel = functools.partial(force_kernel, weight, keep, shift, send, whole)
        base = () if weight is None else (base,)
        terms = given if whole else table
        return call(kernel, outs, (flags, terms), (vb, part, *received, coeffs, *base), ext)

    h, gaps = step_size, node_gaps
    vb, *packs = call(first_kernel, [rounded] + rims, (flags,), (first,))
    received = exchange(packs)
    split = jax.ShapeDtypeStruct((species, 3 * species), bf16)
    part, mix, coeffs = pl.pallas_call(
        first_reaction_kernel,
        out_shape=[state, split, jax.ShapeDtypeStruct(coeffs.shape, bf16)],
        in_specs=[VMEM, VMEM, pl.BlockSpec(memory_space=pltpu.HBM)],
        out_specs=[VMEM] * 3,
        scratch_shapes=[pltpu.SemaphoreType.DMA],
        compiler_params=pltpu.CompilerParams(vmem_limit_bytes=48 * 1024 * 1024),
        cost_estimate=pl.CostEstimate(flops=4_000_000, bytes_accessed=4_000_000, transcendentals=0),
    )(first, mixing, coeffs)
    f, fb = force(received, vb, part, shift=True, whole=True)
    table, mark = pl.pallas_call(
        table_kernel,
        out_shape=[jax.ShapeDtypeStruct((nblocks * WIDTH + 1,), jnp.int32), jax.ShapeDtypeStruct((8, 128), f32)],
        in_specs=[SMEM, VMEM],
        out_specs=[SMEM, VMEM],
        compiler_params=PARAMS,
        cost_estimate=pl.CostEstimate(flops=1_000_000, bytes_accessed=1_000_000, transcendentals=0),
    )(given, f)

    arrays = (first, next_slice(first), f, next_slice(fb))
    received = exchange(moved_packs(early_step, arrays))
    part, base, vb, e0 = move_and_prepare(early_step, arrays, prepare_first(1), (f,), True)
    e1, u, vb, *packs = force(received, vb, part, h * gaps[1], base, send=True)

    received = exchange(packs)
    part, base = react_and_prepare(u, vb, prepare_first(2), (f,))
    e2, u, vb, *packs = force(received, vb, part, h * gaps[2], base, send=True)

    came = next_slice(u)
    received = exchange(packs)
    part, base = react_and_prepare(u, vb, prepare_late, (e0, e1, e2))
    e3, e3b, olds = force(received, vb, part, h * node_integrals[0][2], base, shift=True)

    arrays = (first, came, e0, next_slice(e3b), olds)
    received = exchange(moved_packs(late_step, arrays))
    olds = (e1, e2, e3)
    part, base, vb = move_and_prepare(late_step, arrays, prepare_second(1), olds, False)
    u, vb, *packs = force(received, vb, part, h * gaps[1], base, keep=False, send=True)

    received = exchange(packs)
    part, base = react_and_prepare(u, vb, prepare_second(2), olds)
    (end,) = force(received, vb, part, h * gaps[2], base, keep=False)
    return jnp.transpose(end, (1, 0, 2))[None]


def solution(mesh):
    placed = (
        P("tm", None, "space", None),
        P(),
        P("space", None),
        P("space", None),
        P("space", None),
        P(),
    )
    return jax.shard_map(
        per_device,
        mesh=mesh,
        in_specs=placed,
        out_specs=P("tm", None, "space", None),
        check_vma=False,
    )
```

```python
import functools
import math

import jax
import jax.numpy as jnp
from jax import lax
from jax.experimental import pallas as pl
from jax.experimental.pallas import tpu as pltpu
from jax.sharding import PartitionSpec as P

SWEEPS = 2

step_size = 0.3
root_six = math.sqrt(6.0)
node_times = ((4.0 - root_six) / 10.0, (4.0 + root_six) / 10.0, 1.0)
radau_rows = (
    (
        (88.0 - 7.0 * root_six) / 360.0,
        (296.0 - 169.0 * root_six) / 1800.0,
        (-2.0 + 3.0 * root_six) / 225.0,
    ),
    (
        (296.0 + 169.0 * root_six) / 1800.0,
        (88.0 + 7.0 * root_six) / 360.0,
        (-2.0 - 3.0 * root_six) / 225.0,
    ),
    ((16.0 - root_six) / 36.0, (16.0 + root_six) / 36.0, 1.0 / 9.0),
)
node_gaps = (node_times[0], node_times[1] - node_times[0], node_times[2] - node_times[1])
node_integrals = (
    radau_rows[0],
    tuple((radau_rows[1][j] - radau_rows[0][j] for j in range(3))),
    tuple((radau_rows[2][j] - radau_rows[1][j] for j in range(3))),
)

f32 = jnp.float32
bf16 = jnp.bfloat16
VMEM = pl.BlockSpec(memory_space=pltpu.VMEM)
SMEM = pl.BlockSpec(memory_space=pltpu.SMEM)
PARAMS = pltpu.CompilerParams(vmem_limit_bytes=8 * 1024 * 1024)
UNROLL = 32
TERMS = 8
WIDTH = 2 * TERMS


def pairing(slices, parts, distance, late):
    route = []
    for a in range(slices):
        for p in range(parts):
            ahead = ((p // distance) % 2 == 0) != late
            q = p + distance if ahead else p - distance
            b, q = (a, q) if 0 <= q < parts else (a ^ 1, p)
            route.append((a * parts + p, b * parts + q))
    return route


def swap(block, distance, late):
    route = pairing(lax.axis_size("tm"), lax.axis_size("space"), distance, late)
    return lax.ppermute(block, ("tm", "space"), route)


def next_slice(block):
    n = lax.axis_size("tm")
    return lax.ppermute(block, "tm", [(i, (i + 1) % n) for i in range(n)])


PLAN = 13
PAIRS = ((2, True), (2, False), (1, True), (1, False))


def exchange(packs):
    return tuple(swap(x, d, late) for x, (d, late) in zip(packs, PAIRS))


def plan():
    p = lax.axis_index("space")
    n = lax.axis_size("space")
    sends, fills, valid = [], [], []
    for distance, late in PAIRS:
        base = 0 if distance == 1 else 2
        ahead = ((p // distance) % 2 == 0) != late
        q = jnp.where(ahead, p + distance, p - distance)
        sends.append(jnp.where(ahead, base, base + 1))
        fills.append(jnp.where(ahead, base + 1, base))
        valid.append((q >= 0) & (q < n))
    leading = lax.axis_index("tm") == 0
    return jnp.stack([x.astype(jnp.int32) for x in sends + fills + valid + [leading]])


def pack(flags, vb, packs):
    slots = packs[0].shape[0]
    for k, out in enumerate(packs):
        first = PLAN + flags[k] * slots
        for j in range(slots):
            out[j] = vb[flags[first + j]]


def first_kernel(flags, guess, u, vb, *packs):
    nblocks, species, _ = u.shape

    def body(b):
        field = guess[pl.ds(b, species, stride=nblocks), :]
        u[b] = field
        vb[b] = field.astype(bf16)

    per_block(nblocks, body)
    vb[nblocks] = jnp.zeros(vb.shape[1:], bf16)
    pack(flags, vb, packs)


def react(mix, field):
    th = jnp.tanh(field)
    hi = th.astype(bf16)
    lo = (th - hi.astype(f32)).astype(bf16)
    return jnp.dot(mix, jnp.concatenate([hi, hi, lo], axis=0), preferred_element_type=f32)


def per_block(count, body):
    def several(i, carry):
        for j in range(UNROLL):
            body(i * UNROLL + j)
        return carry

    lax.fori_loop(0, count // UNROLL, several, 0)


def local_terms(table, coeffs, vb, b):
    nblocks = vb.shape[0] - 1
    at = b * WIDTH
    other = jnp.minimum(table[at + TERMS], nblocks)
    return jnp.dot(
        jnp.concatenate([vb[b], vb[other]], axis=1),
        jnp.concatenate([coeffs[table[at]], coeffs[table[at + 1]]], axis=0),
        preferred_element_type=f32,
    )


def first_reaction_kernel(u, mixing, coeffs, part, mix, matrices, arrival):
    fetch = pltpu.make_async_copy(coeffs, matrices, arrival)
    fetch.start()
    m = mixing[...]
    m_hi = m.astype(bf16)
    m_lo = (m - m_hi.astype(f32)).astype(bf16)
    mix[...] = jnp.concatenate([m_hi, m_lo, m_hi], axis=1)
    mixv = mix[...]

    def body(b):
        part[b] = react(mixv, u[b])

    per_block(u.shape[0], body)
    fetch.wait()


def table_kernel(given, after, table, mark):
    nblocks = after.shape[0]
    mark[...] = jnp.zeros_like(mark)

    def body(b, count):
        source, at = b * (WIDTH - 1), b * WIDTH
        values = [given[source + t] for t in range(WIDTH - 1)]
        mats, cols = values[1:TERMS], values[TERMS:]
        chosen, mat, col = jnp.int32(TERMS), mats[0], cols[0]
        for t in reversed(range(TERMS - 1)):
            local = cols[t] < nblocks
            chosen = jnp.where(local, t, chosen)
            mat = jnp.where(local, mats[t], mat)
            col = jnp.where(local, cols[t], col)
        lonely = chosen == TERMS
        chosen = jnp.where(lonely, 0, chosen)
        table[at] = values[0]
        for t in range(1, TERMS - 1):
            table[at + 1 + t] = mats[t]
            table[at + TERMS + t] = cols[t]
        table[at + 1 + chosen] = mats[0]
        table[at + TERMS + chosen] = cols[0]
        table[at + 1] = mat
        table[at + TERMS] = col
        table[count * WIDTH + WIDTH - 1] = b
        return count + lonely.astype(jnp.int32)

    table[nblocks * WIDTH] = lax.fori_loop(0, nblocks, body, jnp.int32(0), unroll=4)


def reaction_kernel(prepare, extras, table, u, vb, mix, coeffs, *refs):
    olds, (part, base) = refs[:extras], refs[extras:]
    mixv = mix[...]

    def body(b):
        field = u[b]
        part[b] = react(mixv, field) + local_terms(table, coeffs, vb, b)
        base[b] = prepare(field, [old[b] for old in olds])

    per_block(u.shape[0], body)


def moved_pack_kernel(step, extras, flags, mark, *refs):
    del mark
    arrays, packs = refs[:extras], refs[extras:]
    nblocks = arrays[0].shape[0]
    slots = packs[0].shape[0]
    leading = flags[PLAN - 1] > 0

    def fill(lead):
        for k, out in enumerate(packs):
            first = PLAN + flags[k] * slots
            for j in range(slots):
                row = flags[first + j]
                block = step(lead, arrays, jnp.minimum(row, nblocks - 1))[0].astype(bf16)
                out[j] = jnp.where(row < nblocks, block, jnp.zeros_like(block))

    pl.when(leading)(lambda: fill(True))
    pl.when(jnp.logical_not(leading))(lambda: fill(False))


def moved_reaction_kernel(step, prepare, extras, inputs, keep, flags, table, mix, coeffs, *refs):
    arrays, olds, outs = refs[:extras], refs[extras:inputs], refs[inputs:]
    part, base, vb = outs[:3]
    nblocks = part.shape[0]
    leading = flags[PLAN - 1] > 0
    mixv = mix[...]
    vb[nblocks] = jnp.zeros(vb.shape[1:], bf16)

    def body(b):
        field, force = step(leading, arrays, b)
        if keep:
            outs[3][b] = force
        vb[b] = field.astype(bf16)
        part[b] = react(mixv, field)
        base[b] = prepare(field, [old[b] for old in olds])

    def add(b):
        part[b] += local_terms(table, coeffs, vb, b)

    per_block(nblocks, body)
    per_block(nblocks, add)


def force_kernel(weight, keep, shift, send, whole, flags, table, vb, part, *refs):
    received, refs = refs[:4], refs[4:]
    coeffs, refs = refs[0], refs[1:]
    if weight is not None:
        base, refs = refs[0], refs[1:]
    outs, ext = list(refs[:-1]), refs[-1]
    forces = outs.pop(0) if keep else None
    shifted = outs.pop(0) if shift else None
    states = outs.pop(0) if weight is not None else None
    rounded = outs.pop(0) if send else None
    nblocks = part.shape[0]
    slots = received[0].shape[0]
    ext[0:nblocks] = vb[0:nblocks]
    for k, got in enumerate(received):
        live = flags[8 + k] > 0
        block = got[...]
        ext[pl.ds(nblocks + flags[4 + k] * slots, slots)] = jnp.where(live, block, jnp.zeros_like(block))

    def body(b):
        if whole:
            at = b * (WIDTH - 1)
            xs = [vb[b]] + [ext[table[at + TERMS + t]] for t in range(TERMS - 1)]
            ws = [coeffs[table[at + t]] for t in range(TERMS)]
        else:
            at = b * WIDTH
            xs = [ext[table[at + TERMS + t]] for t in range(1, TERMS - 1)]
            ws = [coeffs[table[at + 1 + t]] for t in range(1, TERMS - 1)]
        force = part[b] + jnp.dot(
            jnp.concatenate(xs, axis=1), jnp.concatenate(ws, axis=0), preferred_element_type=f32
        )
        if keep:
            forces[b] = force
        if shift:
            shifted[b] = force.astype(bf16)
        if weight is not None:
            new = base[b] + weight * force
            states[b] = new
            if send:
                rounded[b] = new.astype(bf16)

    def late(i, carry):
        b = table[i * WIDTH + WIDTH - 1]
        at = b * WIDTH
        more = jnp.dot(ext[table[at + TERMS]], coeffs[table[at + 1]], preferred_element_type=f32)
        if keep:
            force = forces[b] + more
            forces[b] = force
            if shift:
                shifted[b] = force.astype(bf16)
        if weight is not None:
            new = states[b] + weight * more
            states[b] = new
            if send:
                rounded[b] = new.astype(bf16)
        return carry

    per_block(nblocks, body)
    if not whole:
        lax.fori_loop(0, table[nblocks * WIDTH], late, 0)
    if send:
        rounded[nblocks] = jnp.zeros(rounded.shape[1:], bf16)
        pack(flags, rounded, outs)


def pick(which, one, other):
    if isinstance(which, bool):
        return one() if which else other()
    return jnp.where(which, one(), other())


def early_step(leading, arrays, b):
    guess, incoming, force, moved = arrays
    g, q = node_gaps[0], sum(node_integrals[0])
    f = force[b]
    start = pick(leading, lambda: guess[b], lambda: incoming[b])
    e = pick(leading, lambda: f, lambda: moved[b].astype(f32))
    return start + step_size * (g * (e - f) + q * f), e


def late_step(leading, arrays, b):
    guess, incoming, force, moved, olds = arrays
    start = pick(leading, lambda: guess[b], lambda: incoming[b])
    e = pick(leading, lambda: force[b], lambda: moved[b].astype(f32))
    return start + olds[b] + (step_size * node_gaps[0]) * e, e


def prepare_first(node):
    g, q = node_gaps[node], sum(node_integrals[node])

    def prepare(u, olds):
        (f,) = olds
        return u + step_size * (q * f - g * f)

    return prepare


def prepare_second(node):
    g, q = node_gaps[node], node_integrals[node]

    def prepare(u, olds):
        quad = q[0] * olds[0] + q[1] * olds[1] + q[2] * olds[2]
        return u + step_size * (quad - g * olds[node - 1])

    return prepare


def prepare_late(u, olds):
    e0, e1, e2 = olds
    q = node_integrals[0]
    return step_size * (q[0] * e1 + q[1] * e2 - node_gaps[0] * e0)


def per_device(guess, coeffs, coef_index, neighbours, send_lists, mixing):
    species, nblocks, cells = guess.shape[1:]
    slots = send_lists.shape[1]
    rows = jnp.where(send_lists < 0, nblocks, send_lists)
    flags = jnp.concatenate([plan(), rows.reshape(-1)])
    given = jnp.concatenate([coef_index, neighbours], axis=1).reshape(-1)

    state = jax.ShapeDtypeStruct((nblocks, species, cells), f32)
    shifted = jax.ShapeDtypeStruct((nblocks, species, cells), bf16)
    rounded = jax.ShapeDtypeStruct((nblocks + 1, species, cells), bf16)
    rims = [jax.ShapeDtypeStruct((slots, species, cells), bf16)] * 4
    ext = [pltpu.VMEM((nblocks + 4 * slots, species, cells), bf16)]

    def call(kernel, outs, scalars, arrays, scratch=(), cost=4_000_000):
        return pl.pallas_call(
            kernel,
            out_shape=outs,
            in_specs=[SMEM] * len(scalars) + [VMEM] * len(arrays),
            out_specs=[VMEM] * len(outs),
            scratch_shapes=scratch,
            compiler_params=PARAMS,
            cost_estimate=pl.CostEstimate(flops=cost, bytes_accessed=cost, transcendentals=0),
        )(*scalars, *arrays)

    def react_and_prepare(u, vb, prepare, olds):
        kernel = functools.partial(reaction_kernel, prepare, len(olds))
        return call(kernel, [state, state], (table,), (u, vb, mix, coeffs, *olds))

    def move_and_prepare(step, arrays, prepare, olds, keep):
        inputs = len(arrays) + len(olds)
        kernel = functools.partial(moved_reaction_kernel, step, prepare, len(arrays), inputs, keep)
        outs = [state, state, rounded] + [state] * keep
        return call(kernel, outs, (flags, table), (mix, coeffs, *arrays, *olds))

    def moved_packs(step, arrays):
        kernel = functools.partial(moved_pack_kernel, step, len(arrays))
        return call(kernel, rims, (flags,), (mark, *arrays))

    def force(received, vb, part, weight=None, base=None, keep=True, shift=False, send=False, whole=False):
        outs = [state] * keep + [shifted] * shift + [state] * (weight is not None)
        if send:
            outs += [rounded] + rims
        kernel = functools.partial(force_kernel, weight, keep, shift, send, whole)
        base = () if weight is None else (base,)
        terms = given if whole else table
        return call(kernel, outs, (flags, terms), (vb, part, *received, coeffs, *base), ext)

    h, gaps = step_size, node_gaps
    first, vb, *packs = call(
        first_kernel, [state, rounded] + rims, (flags,), (guess.reshape(species * nblocks, cells),)
    )
    received = exchange(packs)
    split = jax.ShapeDtypeStruct((species, 3 * species), bf16)
    part, mix, coeffs = pl.pallas_call(
        first_reaction_kernel,
        out_shape=[state, split, jax.ShapeDtypeStruct(coeffs.shape, bf16)],
        in_specs=[VMEM, VMEM, pl.BlockSpec(memory_space=pltpu.HBM)],
        out_specs=[VMEM] * 3,
        scratch_shapes=[pltpu.SemaphoreType.DMA],
        compiler_params=pltpu.CompilerParams(vmem_limit_bytes=48 * 1024 * 1024),
        cost_estimate=pl.CostEstimate(flops=4_000_000, bytes_accessed=4_000_000, transcendentals=0),
    )(first, mixing, coeffs)
    f, fb = force(received, vb, part, shift=True, whole=True)
    table, mark = pl.pallas_call(
        table_kernel,
        out_shape=[jax.ShapeDtypeStruct((nblocks * WIDTH + 1,), jnp.int32), jax.ShapeDtypeStruct((8, 128), f32)],
        in_specs=[SMEM, VMEM],
        out_specs=[SMEM, VMEM],
        compiler_params=PARAMS,
        cost_estimate=pl.CostEstimate(flops=1_000_000, bytes_accessed=1_000_000, transcendentals=0),
    )(given, f)

    arrays = (first, next_slice(first), f, next_slice(fb))
    received = exchange(moved_packs(early_step, arrays))
    part, base, vb, e0 = move_and_prepare(early_step, arrays, prepare_first(1), (f,), True)
    e1, u, vb, *packs = force(received, vb, part, h * gaps[1], base, send=True)

    received = exchange(packs)
    part, base = react_and_prepare(u, vb, prepare_first(2), (f,))
    e2, u, vb, *packs = force(received, vb, part, h * gaps[2], base, send=True)

    came = next_slice(u)
    received = exchange(packs)
    part, base = react_and_prepare(u, vb, prepare_late, (e0, e1, e2))
    e3, e3b, olds = force(received, vb, part, h * node_integrals[0][2], base, shift=True)

    arrays = (first, came, e0, next_slice(e3b), olds)
    received = exchange(moved_packs(late_step, arrays))
    olds = (e1, e2, e3)
    part, base, vb = move_and_prepare(late_step, arrays, prepare_second(1), olds, False)
    u, vb, *packs = force(received, vb, part, h * gaps[1], base, keep=False, send=True)

    received = exchange(packs)
    part, base = react_and_prepare(u, vb, prepare_second(2), olds)
    (end,) = force(received, vb, part, h * gaps[2], base, keep=False)
    return jnp.transpose(end, (1, 0, 2))[None]


def solution(mesh):
    placed = (
        P("tm", None, "space", None),
        P(),
        P("space", None),
        P("space", None),
        P("space", None),
        P(),
    )
    return jax.shard_map(
        per_device,
        mesh=mesh,
        in_specs=placed,
        out_specs=P("tm", None, "space", None),
        check_vma=False,
    )
```
